128 devices in a mesh: dp: 16 (over y, x), expert: 8 (over z, core).
Axes of the slice: x: 4, y: 4, z: 4, core: 2. Of those that a mesh axis runs over, the one named last changes fastest.
Arguments:
- tokens: bfloat16 [16384, 1280], P(('dp', 'expert')), may hold values from -6 to 6
- cotangent: bfloat16 [16384, 1280], P(('dp', 'expert')), may hold values from -4 to 4
- gate_weights: float32 [16384, 2], P(('dp', 'expert')), may hold values from 0.1 to 1
- expert_ids: int32 [16384, 2], P(('dp', 'expert')), may hold values from 0 to 15, as said below
- segments: int32 [128, 128], P(('dp', 'expert')), may hold values from 0 to 3, never falling along the last dimension, each value on 1 to 64 neighbouring positions
- keep_counts: int32 [128, 4], P(('dp', 'expert')), may hold values from 1 to 64
- expand_weight: bfloat16 [16, 2560, 1280], P('expert', 'dp'), may hold values from -0.15625 to 0.15625
- reduce_weight: bfloat16 [16, 2560, 1280], P('expert', 'dp'), may hold values from -0.125 to 0.125
Outputs:
- output: bfloat16 [16384, 1280], P(('dp', 'expert'))
- tokens_grad: bfloat16 [16384, 1280], P(('dp', 'expert'))
- gating_grad: float32 [16384, 2], P(('dp', 'expert'))
- expand_grad: bfloat16 [16, 2560, 1280], P('expert', 'dp')
- reduce_grad: bfloat16 [16, 2560, 1280], P('expert', 'dp')
The draws below stay inside these ranges and needn't reach their ends.
Inputs may be any that keep to these rules, and one draw needn't show every extreme that they name: `expert_ids`: the 128 tokens of one sequence name each expert exactly 16 times, and a token's 2 experts differ. `segments`: within a sequence the ids never fall, every image 0 to 3 appears, each holds 1 to 64 positions.
All inputs are finite; a program needn't handle non-finite values.
Results may differ from the reference program's by a relative error of at most 0.015.
Values may be sent and summed in bfloat16 or wider, within the bound.
A program may use at most 128 MiB of HBM per device.

```python
import math
import jax
import jax.numpy as jnp
import numpy as np
from jax import lax

D = 1280
H = 2560
TOP = 2
IMGS = 4
TOK_DEV = 128
E = 16
SEG_MOST = 64
SEQS = 128
TOKENS = 16384
N_DP = 16
N_EXPERT = 8


def route_block(block_key):
    label_key, shift_key, flip_key, order_key = jax.random.split(block_key, 4)
    labels = jax.random.permutation(label_key, jnp.arange(E, dtype=jnp.int32))
    rounds = TOK_DEV // E
    shifts = jax.random.randint(shift_key, (rounds,), 1, E, dtype=jnp.int32)
    row_index = jnp.arange(TOK_DEV, dtype=jnp.int32)
    first_label = row_index % E
    second_label = (first_label + shifts[row_index // E]) % E
    first_ids = labels[first_label]
    second_ids = labels[second_label]
    flips = jax.random.randint(flip_key, (TOK_DEV,), 0, 2, dtype=jnp.int32)
    column_zero = jnp.where(flips == 1, second_ids, first_ids)
    column_one = jnp.where(flips == 1, first_ids, second_ids)
    paired = jnp.stack([column_zero, column_one], axis=1)
    order = jax.random.permutation(order_key, jnp.arange(TOK_DEV, dtype=jnp.int32))
    return paired[order]


def draw_expert_ids(key, part):
    block_keys = jax.random.split(jax.random.fold_in(key, 7), SEQS)
    blocks = jax.vmap(route_block)(block_keys)
    return blocks.reshape(TOKENS, TOP).astype(jnp.int32)


def touch_ends(values, stream_key, smallest, top_value):
    extent = values.shape
    spot = [jax.random.randint(jax.random.fold_in(stream_key, axis), (), 0, extent[axis]) for axis in range(len(extent))]
    values = values.at[tuple(spot)].set(smallest)
    longest = extent.index(max(extent))
    spot[longest] = (spot[longest] + 1) % extent[longest]
    return values.at[tuple(spot)].set(top_value)


def levels(key, shape, shards, smallest, largest):
    level = 1.0
    for dim, blocks in shards:
        steps = jax.random.uniform(jax.random.fold_in(jax.random.fold_in(key, 6), dim), (blocks,), jnp.float32, smallest / len(shards), largest / len(shards))
        level = level * jnp.repeat(jnp.exp(steps), shape[dim] // blocks).reshape((-1,) + (1,) * (len(shape) - 1 - dim))
    return level


def length_profile(count, total, most, lean):
    portions = [(1 << 20) // math.isqrt(rank ** lean) + 1 for rank in range(2, count + 1)]
    rest, holding = total - most - (count - 1), [1] * (count - 1)
    while rest > 0:
        movable = [i for i in range(count - 1) if holding[i] < most]
        whole, left = sum([portions[i] for i in movable]), rest
        for i in movable:
            more = min(most - holding[i], max(1, left * portions[i] // whole), rest)
            holding[i] = holding[i] + more
            rest = rest - more
    return np.array([most] + holding)


def ragged(own_key, number_of, total, most, slope):
    if number_of == 2:
        one = jax.random.randint(own_key, (), max(1, total - most), min(most, total - 1) + 1)
        return jnp.stack([one, total - one])
    tallies = jnp.asarray(length_profile(number_of, total, most, slope), jnp.int32)
    couples = (number_of - 1) // 2
    giver, receiver = tallies[1:1 + 2 * couples:2], tallies[2:2 + 2 * couples:2]
    margin = jnp.minimum(giver - 1, most - receiver)
    shifted = jax.random.randint(jax.random.fold_in(own_key, 1), (couples,), 0, 1 << 20) % (margin + 1)
    tallies = tallies.at[1:1 + 2 * couples:2].set(giver - shifted).at[2:2 + 2 * couples:2].set(receiver + shifted)
    return tallies[jax.random.permutation(jax.random.fold_in(own_key, 2), number_of)]


def noise(stream_key, extent, spread, reach, pieces=(), kind=jnp.bfloat16):
    loudness = levels(stream_key, extent, pieces, -0.22, 0.18) if pieces else 1.0
    drawn = jax.random.normal(stream_key, extent, jnp.float32) * spread * loudness
    return jnp.minimum(jnp.maximum(drawn, -reach), reach).astype(kind)


def setup_inputs(seed: int = 0) -> dict:
    streams_of = jax.random.split(jax.random.key(seed), 9)
    return {
        "tokens": noise(streams_of[0], (TOKENS, D), 1.0, 6.0, ((0, 128),)),
        "cotangent": noise(streams_of[1], (TOKENS, D), 0.3, 4.0, ((0, 128),)),
        "gate_weights": jnp.clip(0.1 + 0.9 * jax.random.uniform(streams_of[2], (TOKENS, TOP), jnp.float32) ** levels(streams_of[2], (TOKENS, TOP), ((0, 128),), -0.2, 0.2), 0.1, 1.0),
        "expert_ids": draw_expert_ids(jax.random.fold_in(streams_of[8], 71), 0),
        "segments": jax.vmap(lambda own: jnp.searchsorted(jnp.cumsum(ragged(own, IMGS, TOK_DEV, SEG_MOST, 1)), jnp.arange(TOK_DEV), side="right"))(jax.random.split(streams_of[4], SEQS)).reshape((SEQS, TOK_DEV)).astype(jnp.int32),
        "keep_counts": touch_ends(jax.random.randint(streams_of[5], (SEQS, IMGS), 1, SEG_MOST + 1), jax.random.fold_in(streams_of[5], 1), 1, SEG_MOST).astype(jnp.int32),
        "expand_weight": noise(streams_of[6], (E, H, D), D ** -0.5, 0.15625, ((0, 8), (1, 16))),
        "reduce_weight": noise(streams_of[7], (E, H, D), H ** -0.5, 0.125, ((0, 8), (1, 16))),
    }


epsilon = 1e-06
root_half = 0.7071067811865476
density_scale = 0.3989422804014327

def gelu_value(values):
    return 0.5 * values * (1.0 + jax.scipy.special.erf(values * root_half))

def gelu_slope(values):
    return 0.5 * (1.0 + jax.scipy.special.erf(values * root_half)) + values * jnp.exp(-0.5 * values * values) * density_scale

def round_partials(partials):
    return lax.optimization_barrier(partials.astype(jnp.bfloat16)).astype(jnp.float32)

def reference(tokens, cotangent, gate_weights, expert_ids, segments, keep_counts, expand_weight, reduce_weight):
    device_count = N_DP * N_EXPERT
    capacity = TOP * TOK_DEV // E
    position = jnp.arange(TOK_DEV, dtype=jnp.int32)
    earlier_img = lax.optimization_barrier(jnp.sum((segments[:, None, :] < segments[:, :, None]).astype(jnp.int32), axis=2))
    keep_token = jnp.take_along_axis(keep_counts, segments, axis=1)
    alive = (position[None, :] - earlier_img < keep_token).astype(jnp.float32).reshape(-1)
    tokens_wide = tokens.astype(jnp.float32)
    mean_rows = lax.optimization_barrier(jnp.mean(tokens_wide, axis=1, keepdims=True))
    centred = tokens_wide - mean_rows
    inv_scale = lax.rsqrt(lax.optimization_barrier(jnp.mean(centred * centred, axis=1, keepdims=True)) + epsilon)
    normed = centred * inv_scale
    normed_low = normed.astype(jnp.bfloat16)
    choice_list = expert_ids.reshape(device_count, TOP * TOK_DEV)
    matches = (choice_list[:, :, None] == jnp.arange(E, dtype=jnp.int32)[None, None, :]).astype(jnp.int32)
    before = jnp.cumsum(matches, axis=1) - matches
    slot_list = lax.optimization_barrier(jnp.sum(before * matches, axis=2)).reshape(-1).astype(jnp.int32)
    choice_flat = choice_list.reshape(-1).astype(jnp.int32)
    device_flat = jnp.repeat(jnp.arange(device_count, dtype=jnp.int32), TOP * TOK_DEV)
    alive_pick = jnp.repeat(alive, TOP)
    weight_pick = gate_weights.reshape(-1) * alive_pick
    feature_rows = jnp.where(alive_pick[:, None] > 0, jnp.repeat(normed_low, TOP, axis=0), jnp.zeros((), jnp.bfloat16))
    grad_rows = (jnp.repeat(cotangent.astype(jnp.float32), TOP, axis=0) * weight_pick[:, None]).astype(jnp.bfloat16)
    routed = jnp.zeros((device_count, E, capacity, D), jnp.bfloat16).at[device_flat, choice_flat, slot_list].set(feature_rows)
    routed_grad = jnp.zeros((device_count, E, capacity, D), jnp.bfloat16).at[device_flat, choice_flat, slot_list].set(grad_rows)

    def per_expert(inputs):
        features, grads, first, second = inputs
        features = features.reshape(-1, D)
        grads = grads.reshape(-1, D)
        pre = jnp.dot(features, first.T, preferred_element_type=jnp.float32)
        hidden = gelu_value(pre).astype(jnp.bfloat16)
        result = jnp.dot(hidden, second, preferred_element_type=jnp.float32).astype(jnp.bfloat16)
        back_hidden = jnp.dot(grads, second.T, preferred_element_type=jnp.float32)
        dpre = (back_hidden * gelu_slope(pre)).astype(jnp.bfloat16)
        input_rows = jnp.dot(dpre, first, preferred_element_type=jnp.float32).astype(jnp.bfloat16)
        hidden_blocks = hidden.reshape(N_DP, -1, H).astype(jnp.float32)
        dpre_blocks = dpre.reshape(N_DP, -1, H).astype(jnp.float32)
        grad_blocks = grads.reshape(N_DP, -1, D).astype(jnp.float32)
        feature_blocks = features.reshape(N_DP, -1, D).astype(jnp.float32)
        second_parts = jnp.einsum('bsh,bsd->bhd', hidden_blocks, grad_blocks)
        first_parts = jnp.einsum('bsh,bsd->bhd', dpre_blocks, feature_blocks)
        second_grad = lax.optimization_barrier(jnp.sum(round_partials(second_parts), axis=0)).astype(jnp.bfloat16)
        first_grad = lax.optimization_barrier(jnp.sum(round_partials(first_parts), axis=0)).astype(jnp.bfloat16)
        return (result, input_rows, first_grad, second_grad)
    results, input_grads, expand_grad, reduce_grad = lax.map(per_expert, (routed.transpose(1, 0, 2, 3), routed_grad.transpose(1, 0, 2, 3), expand_weight, reduce_weight))
    results = results.reshape(E, device_count, capacity, D)
    input_grads = input_grads.reshape(E, device_count, capacity, D)
    result_pick = results[choice_flat, device_flat, slot_list].astype(jnp.float32).reshape(-1, TOP, D)
    input_pick = input_grads[choice_flat, device_flat, slot_list].astype(jnp.float32).reshape(-1, TOP, D)
    output = (tokens_wide + lax.optimization_barrier(jnp.sum(result_pick * weight_pick.reshape(-1, TOP, 1), axis=1))).astype(jnp.bfloat16)
    cot_wide = cotangent.astype(jnp.float32)
    gating_grad = alive_pick.reshape(-1, TOP) * lax.optimization_barrier(jnp.sum(cot_wide[:, None, :] * result_pick, axis=2))
    grad_norm = lax.optimization_barrier(jnp.sum(input_pick * alive_pick.reshape(-1, TOP, 1), axis=1))
    tokens_grad = cot_wide + inv_scale * (grad_norm - lax.optimization_barrier(jnp.mean(grad_norm, axis=1, keepdims=True)) - normed * lax.optimization_barrier(jnp.mean(grad_norm * normed, axis=1, keepdims=True)))
    return (output, tokens_grad.astype(jnp.bfloat16), gating_grad, expand_grad, reduce_grad)
```

```python
import jax
import jax.numpy as jnp
from jax import lax
from jax.experimental import pallas as pl
from jax.experimental.pallas import tpu as pltpu
from jax.sharding import PartitionSpec as P

MESH = pl.DeviceIdType.MESH
epsilon = 1e-06
root_half = 0.7071067811865476
density_scale = 0.3989422804014327

D = 1280
TOK = 128
SLOTS = 256
CAP = 16
NE = 16
SH = 160
HS = SH // 2
Q = 4 * HS
HID = 4 * Q
ROWS = 2 * SLOTS
BF = jnp.bfloat16
F32 = jnp.float32


def dot(a, b, ca, cb):
    return lax.dot_general(a, b, (((ca,), (cb,)), ((), ())), preferred_element_type=F32)


def kernel(
    tok, cot, gw, ids, seg, keep, w1_in, w2_in,
    out, tg, gg, eg, rg,
    pt, normed, inv, wcol, acol, xs, gs, x_all, g_all, w1, w2, hid, slope, dpre, trans,
    y_send, y_own, y_recv, y_fin, y_ret, d_send, d_own, d_recv, d_fin, d_ret,
    e_own, e_send, e_core, e_wp, e_far, e_fin, r_own, r_send, r_core, r_wp, r_far, r_fin,
    a_ss, a_rs, b_ss, b_rs, w_ss, w_rs, wy_ss, wy_rs, wc_ss, wc_rs,
    gc_ss, gc_rs, gy_ss, gy_rs, gx_ss, gx_rs,
):
    dp = lax.axis_index("dp")
    ex = lax.axis_index("expert")
    y, x = dp // 4, dp % 4
    z, c = ex // 2, ex % 2
    me = z * 4 + x
    row_mate = y + 1 - 2 * (y % 2)
    wgt_mate = (y + 5 - 2 * ((y + 1) % 2)) % 4
    other = 1 - c

    def dev(yy, xx, zz, cc):
        return (yy * 4 + xx, zz * 2 + cc)

    row_dev = dev(row_mate, x, z, c)
    wgt_dev = dev(wgt_mate, x, z, c)
    core_dev = dev(y, x, z, other)

    def remote(src, dst, ss, rs, target):
        return pltpu.make_async_remote_copy(
            src_ref=src, dst_ref=dst, send_sem=ss, recv_sem=rs, device_id=target, device_id_type=MESH
        )

    def arrived(dst, rs):
        pltpu.make_async_copy(dst, dst, rs).wait()

    def blk(ref, i, n):
        return ref.at[pl.ds(pl.multiple_of(i * n, n), n)]

    barrier = pltpu.get_barrier_semaphore()
    for i in range(1, NE):
        t = (me + i) % NE
        pl.semaphore_signal(barrier, inc=1, device_id=dev(y, t % 4, t // 4, c), device_id_type=MESH)
    for i in range(4):
        pl.semaphore_signal(barrier, inc=1, device_id=dev(y, i, z, other), device_id_type=MESH)
    for target in (row_dev, wgt_dev):
        pl.semaphore_signal(barrier, inc=1, device_id=target, device_id_type=MESH)
    pl.semaphore_wait(barrier, NE - 1 + 4 + 2)

    def weights_x(m, w_in, w, act):
        for l in range(2):
            for h in range(2):
                tx = 2 * c + l
                src = w_in.at[l, pl.ds(HS * h, HS)]
                dst = blk(w, x, HS)
                own = jnp.logical_and(tx == x, h == c)

                @pl.when(own)
                def _():
                    if act == "start":
                        pltpu.make_async_copy(src, dst, w_rs.at[m, x]).start()

                @pl.when(jnp.logical_not(own))
                def _():
                    copy = remote(src, dst, w_ss.at[m, 2 * l + h], w_rs.at[m, x], dev(y, tx, z, h))
                    copy.start() if act == "start" else copy.wait_send()

    weights_x(0, w1_in, w1, "start")
    weights_x(1, w2_in, w2, "start")

    def swap_blocks(k, src, dst, act):
        if act == "start":
            pltpu.make_async_copy(blk(src, me, CAP), blk(dst, me, CAP), a_rs.at[k, 0]).start()
        for i in range(1, NE):
            t = (me + i) % NE
            copy = remote(
                blk(src, t, CAP), blk(dst, me, CAP), a_ss.at[k, i], a_rs.at[k, i], dev(y, t % 4, t // 4, c)
            )
            copy.start() if act == "start" else copy.wait_send()

    def swap_wait(k, dst):
        for i in range(NE):
            arrived(blk(dst, (me + NE - i) % NE, CAP), a_rs.at[k, i])

    lane = lax.broadcasted_iota(jnp.int32, (TOK, TOK), 1)
    sub = lax.broadcasted_iota(jnp.int32, (TOK, TOK), 0)
    seg_row = jnp.broadcast_to(seg[...].astype(F32), (TOK, TOK))
    seg_col = jnp.sum(jnp.where(lane == sub, seg_row, 0.0), axis=1, keepdims=True)
    earlier = jnp.sum((seg_row < seg_col).astype(F32), axis=1, keepdims=True)
    images = keep.shape[1]
    image = lax.broadcasted_iota(jnp.int32, (TOK, images), 1).astype(F32)
    kept = jnp.broadcast_to(keep[...].astype(F32), (TOK, images))
    keep_token = jnp.sum(jnp.where(image == seg_col, kept, 0.0), axis=1, keepdims=True)
    position = lax.broadcasted_iota(jnp.int32, (TOK, 1), 0).astype(F32)
    alive = (position - earlier < keep_token).astype(F32)
    acol[...] = alive
    wcol[...] = gw[...] * alive
    expert = lax.broadcasted_iota(jnp.int32, (TOK, NE), 1)
    match = [(ids[:, k : k + 1] == expert).astype(F32) for k in range(2)]
    before = dot((lane < sub).astype(BF), (match[0] + match[1]).astype(BF), 1, 0)
    slot_iota = lax.broadcasted_iota(jnp.int32, (TOK, SLOTS), 1).astype(F32)
    for k in range(2):
        slot = jnp.sum(before * match[k], axis=1, keepdims=True)
        if k == 1:
            slot = slot + jnp.sum(match[0] * match[1], axis=1, keepdims=True)
        target_slot = ids[:, k : k + 1].astype(F32) * CAP + slot
        pt[k] = (slot_iota == target_slot).astype(BF)

    wide = tok[...].astype(F32)
    centred = wide - jnp.mean(wide, axis=1, keepdims=True)
    scale = lax.rsqrt(jnp.mean(centred * centred, axis=1, keepdims=True) + epsilon)
    inv[...] = scale
    normed[...] = centred * scale
    feats = (normed[...].astype(BF).astype(F32) * alive).astype(BF)
    xs[...] = dot(pt[0] + pt[1], feats, 0, 0).astype(BF)
    swap_blocks(0, xs, x_all, "start")
    grads = [(cot[...].astype(F32) * wcol[:, k : k + 1]).astype(BF) for k in range(2)]
    gs[...] = (dot(pt[0], grads[0], 0, 0) + dot(pt[1], grads[1], 0, 0)).astype(BF)
    swap_blocks(1, gs, g_all, "start")

    own_rows, mate_rows = pl.ds(0, SLOTS), pl.ds(SLOTS, SLOTS)

    def rows_y(k, src, dst):
        return remote(src, dst, b_ss.at[k], b_rs.at[k], row_dev)

    def quarter(w, s, h):
        return w.at[pl.ds((2 * s + h) * Q, Q)]

    def weights_y(m, w):
        return remote(quarter(w, 0, 0), quarter(w, 1, 0), wy_ss.at[m], wy_rs.at[m], wgt_dev)

    def weights_core(m, w, s):
        return remote(quarter(w, s, 0), quarter(w, s, 1), wc_ss.at[m, s], wc_rs.at[m, s], core_dev)

    def weights_mid(m, w):
        for i in range(4):
            arrived(w.at[pl.ds(i * HS, HS)], w_rs.at[m, i])
        weights_y(m, w).start()
        weights_core(m, w, 0).start()

    def weights_last(m, w):
        weights_y(m, w).wait_recv()
        weights_core(m, w, 1).start()

    swap_wait(0, x_all)
    rows_y(0, x_all.at[own_rows], x_all.at[mate_rows]).start()
    weights_mid(0, w1)
    swap_wait(1, g_all)
    rows_y(1, g_all.at[own_rows], g_all.at[mate_rows]).start()
    weights_mid(1, w2)
    weights_last(0, w1)
    rows_y(0, x_all.at[own_rows], x_all.at[mate_rows]).wait_recv()
    weights_core(0, w1, 0).wait_recv()
    weights_core(0, w1, 1).wait_recv()

    def tile(j, n=256):
        return pl.ds(pl.multiple_of(j * n, n), n)

    @pl.loop(0, HID // 256)
    def _(j):
        pre = dot(x_all[...], w1[tile(j), :], 1, 1)
        cdf = 0.5 * (1.0 + lax.erf(pre * root_half))
        hid[:, tile(j)] = (pre * cdf).astype(BF)
        slope[:, tile(j)] = cdf + pre * jnp.exp(-0.5 * pre * pre) * density_scale

    weights_last(1, w2)
    weights_core(1, w2, 0).wait_recv()
    weights_core(1, w2, 1).wait_recv()

    @pl.loop(0, D // 256)
    def _(n):
        y_send[:, tile(n)] = dot(hid[mate_rows, :], w2[:, tile(n)], 1, 0).astype(BF)

    rows_y(2, y_send, y_recv).start()

    @pl.loop(0, D // 256)
    def _(n):
        y_own[:, tile(n)] = dot(hid[own_rows, :], w2[:, tile(n)], 1, 0)

    rows_y(1, g_all.at[own_rows], g_all.at[mate_rows]).wait_recv()

    @pl.loop(0, HID // 256)
    def _(j):
        back = dot(g_all[...], w2[tile(j), :], 1, 1)
        dpre[:, tile(j)] = (back * slope[:, tile(j)]).astype(BF)

    @pl.loop(0, D // 256)
    def _(n):
        d_send[:, tile(n)] = dot(dpre[mate_rows, :], w1[:, tile(n)], 1, 0).astype(BF)

    rows_y(3, d_send, d_recv).start()

    @pl.loop(0, D // 256)
    def _(n):
        d_own[:, tile(n)] = dot(dpre[own_rows, :], w1[:, tile(n)], 1, 0)

    def rows_back(k, own, send, recv, fin, ret):
        rows_y(k, send, recv).wait_recv()

        @pl.loop(0, SLOTS // 64)
        def _(i):
            fin[tile(i, 64), :] = (own[tile(i, 64), :] + recv[tile(i, 64), :].astype(F32)).astype(BF)

        swap_blocks(k, fin, ret, "start")

    rows_back(2, y_own, y_send, y_recv, y_fin, y_ret)

    def grads_core(m, send, core, s):
        return remote(send.at[s], core.at[s], gc_ss.at[m, s], gc_rs.at[m, s], core_dev)

    def weight_grads(m, left, right, own, send, core):
        @pl.loop(0, HID // 256)
        def _(j):
            trans[tile(j), :] = left[:, tile(j)].T

        for s in (1, 0):

            @pl.loop(0, D // 256)
            def _(n):
                part = dot(trans[pl.ds(s * 2 * Q, 2 * Q), :], right[:, tile(n)], 1, 0)
                own[s, :, tile(n)] = part[:Q]
                send[s, :, tile(n)] = part[Q:].astype(BF)

            grads_core(m, send, core, s).start()

    def grads_y(m, wp, far):
        return remote(wp, far, gy_ss.at[m], gy_rs.at[m], wgt_dev)

    def grads_mid(m, own, send, core, wp, far):
        grads_core(m, send, core, 1).wait_recv()

        @pl.loop(0, Q // 80)
        def _(i):
            wp[tile(i, 80), :] = (own[1, tile(i, 80), :] + core[1, tile(i, 80), :].astype(F32)).astype(BF)

        grads_y(m, wp, far).start()

    def grads_x(m, fin, result, act):
        for i in range(4):
            src = fin.at[pl.ds(i * HS, HS)]
            dst = result.at[x % 2, blk_rows(c)]
            own = jnp.logical_and(i == x, c == x // 2)

            @pl.when(own)
            def _():
                if act == "start":
                    pltpu.make_async_copy(src, dst, gx_rs.at[m, 2 * (x % 2) + c]).start()

            @pl.when(jnp.logical_not(own))
            def _():
                copy = remote(
                    src, dst, gx_ss.at[m, i], gx_rs.at[m, 2 * (x % 2) + c], dev(y, i, z, x // 2)
                )
                copy.start() if act == "start" else copy.wait_send()

    def blk_rows(h):
        return pl.ds(pl.multiple_of(h * HS, HS), HS)

    def grads_last(m, own, send, core, wp, far, fin, result):
        grads_core(m, send, core, 0).wait_recv()
        grads_y(m, wp, far).wait_recv()

        @pl.loop(0, Q // 80)
        def _(i):
            r = tile(i, 80)
            fin[r, :] = (own[0, r, :] + core[0, r, :].astype(F32) + far[r, :].astype(F32)).astype(BF)

        grads_x(m, fin, result, "start")

    weight_grads(1, hid, g_all, r_own, r_send, r_core)
    grads_mid(1, r_own, r_send, r_core, r_wp, r_far)
    rows_back(3, d_own, d_send, d_recv, d_fin, d_ret)
    weight_grads(0, dpre, x_all, e_own, e_send, e_core)
    grads_mid(0, e_own, e_send, e_core, e_wp, e_far)
    grads_last(1, r_own, r_send, r_core, r_wp, r_far, r_fin, rg)

    swap_wait(2, y_ret)
    result = tok[...].astype(F32)
    for k in range(2):
        pick = dot(pt[k], y_ret[...], 1, 0)
        result = result + pick * wcol[:, k : k + 1]
        gg[:, k : k + 1] = acol[...] * jnp.sum(cot[...].astype(F32) * pick, axis=1, keepdims=True)
    out[...] = result.astype(BF)
    swap_wait(3, d_ret)
    dnorm = (dot(pt[0], d_ret[...], 1, 0) + dot(pt[1], d_ret[...], 1, 0)) * acol[...]
    tail = dnorm - jnp.mean(dnorm, axis=1, keepdims=True)
    tail = tail - normed[...] * jnp.mean(dnorm * normed[...], axis=1, keepdims=True)
    tg[...] = (cot[...].astype(F32) + inv[...] * tail).astype(BF)

    grads_last(0, e_own, e_send, e_core, e_wp, e_far, e_fin, eg)

    for m, result in ((1, rg), (0, eg)):
        for l in range(2):
            for h in range(2):
                arrived(result.at[l, pl.ds(h * HS, HS)], gx_rs.at[m, 2 * l + h])
    weights_x(0, w1_in, w1, "wait")
    weights_x(1, w2_in, w2, "wait")
    swap_blocks(0, xs, x_all, "wait")
    swap_blocks(1, gs, g_all, "wait")
    swap_blocks(2, y_fin, y_ret, "wait")
    swap_blocks(3, d_fin, d_ret, "wait")
    rows_y(0, x_all.at[own_rows], x_all.at[mate_rows]).wait_send()
    rows_y(1, g_all.at[own_rows], g_all.at[mate_rows]).wait_send()
    rows_y(2, y_send, y_recv).wait_send()
    rows_y(3, d_send, d_recv).wait_send()
    for m, w in ((0, w1), (1, w2)):
        weights_y(m, w).wait_send()
        for s in range(2):
            weights_core(m, w, s).wait_send()
    for m, send, core, wp, far, fin, result in (
        (0, e_send, e_core, e_wp, e_far, e_fin, eg),
        (1, r_send, r_core, r_wp, r_far, r_fin, rg),
    ):
        for s in range(2):
            grads_core(m, send, core, s).wait_send()
        grads_y(m, wp, far).wait_send()
        grads_x(m, fin, result, "wait")


def body(*args):
    vmem = pl.BlockSpec(memory_space=pltpu.VMEM)
    hbm = pl.BlockSpec(memory_space=pl.ANY)
    dma = pltpu.SemaphoreType.DMA
    shape = jax.ShapeDtypeStruct
    grad_scratch = [
        pltpu.VMEM((2, Q, D), F32),
        pltpu.VMEM((2, Q, D), BF),
        pltpu.VMEM((2, Q, D), BF),
        pltpu.VMEM((Q, D), BF),
        pltpu.VMEM((Q, D), BF),
        pltpu.VMEM((Q, D), BF),
    ]
    row_scratch = [
        pltpu.VMEM((SLOTS, D), BF),
        pltpu.VMEM((SLOTS, D), F32),
        pltpu.VMEM((SLOTS, D), BF),
        pltpu.VMEM((SLOTS, D), BF),
        pltpu.VMEM((SLOTS, D), BF),
    ]
    return pl.pallas_call(
        kernel,
        out_shape=(
            shape((TOK, D), BF),
            shape((TOK, D), BF),
            shape((TOK, 2), F32),
            shape((2, SH, D), BF),
            shape((2, SH, D), BF),
        ),
        in_specs=[vmem] * 6 + [hbm] * 2,
        out_specs=(vmem, vmem, vmem, hbm, hbm),
        scratch_shapes=[
            pltpu.VMEM((2, TOK, SLOTS), BF),
            pltpu.VMEM((TOK, D), F32),
            pltpu.VMEM((TOK, 1), F32),
            pltpu.VMEM((TOK, 2), F32),
            pltpu.VMEM((TOK, 1), F32),
            pltpu.VMEM((SLOTS, D), BF),
            pltpu.VMEM((SLOTS, D), BF),
            pltpu.VMEM((ROWS, D), BF),
            pltpu.VMEM((ROWS, D), BF),
            pltpu.VMEM((HID, D), BF),
            pltpu.VMEM((HID, D), BF),
            pltpu.VMEM((ROWS, HID), BF),
            pltpu.VMEM((ROWS, HID), F32),
            pltpu.VMEM((ROWS, HID), BF),
            pltpu.VMEM((HID, ROWS), BF),
        ]
        + row_scratch * 2
        + grad_scratch * 2
        + [
            dma((4, NE)),
            dma((4, NE)),
            dma((4,)),
            dma((4,)),
            dma((2, 4)),
            dma((2, 4)),
            dma((2,)),
            dma((2,)),
            dma((2, 2)),
            dma((2, 2)),
            dma((2, 2)),
            dma((2, 2)),
            dma((2,)),
            dma((2,)),
            dma((2, 4)),
            dma((2, 4)),
        ],
        compiler_params=pltpu.CompilerParams(
            collective_id=0, has_side_effects=True, vmem_limit_bytes=60 * 2**20
        ),
    )(*args)


def solution(mesh):
    rows = P(("dp", "expert"), None)
    weights = P("expert", "dp", None)
    return jax.shard_map(
        body,
        mesh=mesh,
        in_specs=(rows,) * 6 + (weights,) * 2,
        out_specs=(rows,) * 3 + (weights,) * 2,
        check_vma=False,
    )
```

```python
import jax
import jax.numpy as jnp
from jax import lax
from jax.experimental import pallas as pl
from jax.experimental.pallas import tpu as pltpu
from jax.sharding import PartitionSpec as P

MESH = pl.DeviceIdType.MESH
epsilon = 1e-06
root_half = 0.7071067811865476
density_scale = 0.3989422804014327

D = 1280
TOK = 128
SLOTS = 256
CAP = 16
NE = 16
SH = 160
HS = SH // 2
Q = 4 * HS
HID = 4 * Q
ROWS = 2 * SLOTS
ORDER = (0, 1, 3, 2)
SPANS = ((0, 3), (3, 5))
BF = jnp.bfloat16
F32 = jnp.float32


def dot(a, b, ca, cb):
    return lax.dot_general(a, b, (((ca,), (cb,)), ((), ())), preferred_element_type=F32)


def kernel(
    tok, cot, gw, ids, seg, keep, w1_in, w2_in,
    out, tg, gg, eg, rg,
    pt, normed, inv, wcol, acol, xs, gs, x_all, g_all, w1, w2, hid, slope, dpre, trans,
    y_send, y_recv, y_fin, y_ret, d_send, d_recv, d_fin, d_ret,
    e_own, e_send, e_core, e_wp, e_far, e_fin, r_own, r_send, r_core, r_wp, r_far, r_fin,
    a_ss, a_rs, b_ss, b_rs, p_ss, p_rs, q_ss, q_rs, w_ss, w_rs, wy_ss, wy_rs, wc_ss, wc_rs,
    gc_ss, gc_rs, gy_ss, gy_rs, gx_ss, gx_rs,
):
    dp = lax.axis_index("dp")
    ex = lax.axis_index("expert")
    y, x = dp // 4, dp % 4
    z, c = ex // 2, ex % 2
    row_mate = y + 1 - 2 * (y % 2)
    wgt_mate = (y + 5 - 2 * ((y + 1) % 2)) % 4
    other = 1 - c

    def dev(yy, xx, zz, cc):
        return (yy * 4 + xx, zz * 2 + cc)

    row_dev = dev(row_mate, x, z, c)
    wgt_dev = dev(wgt_mate, x, z, c)
    core_dev = dev(y, x, z, other)

    def remote(src, dst, ss, rs, target):
        return pltpu.make_async_remote_copy(
            src_ref=src, dst_ref=dst, send_sem=ss, recv_sem=rs, device_id=target, device_id_type=MESH
        )

    def arrived(dst, rs):
        pltpu.make_async_copy(dst, dst, rs).wait()

    def part(i, n):
        return pl.ds(pl.multiple_of(i * n, n), n)

    barrier = pltpu.get_barrier_semaphore()
    for dz in range(4):
        for dx in range(4):
            if dz or dx:
                pl.semaphore_signal(
                    barrier, inc=1, device_id=dev(y, (x + dx) % 4, (z + dz) % 4, c), device_id_type=MESH
                )
    for i in range(4):
        pl.semaphore_signal(barrier, inc=1, device_id=dev(y, i, z, other), device_id_type=MESH)
    for target in (row_dev, wgt_dev):
        pl.semaphore_signal(barrier, inc=1, device_id=target, device_id_type=MESH)
    pl.semaphore_wait(barrier, NE - 1 + 4 + 2)

    def weights_x(m, w_in, w, act):
        for l in range(2):
            for h in range(2):
                tx = 2 * c + l
                src = w_in.at[l, pl.ds(HS * h, HS)]
                dst = w.at[part(x, HS)]
                own = jnp.logical_and(tx == x, h == c)

                @pl.when(own)
                def _():
                    if act == "start":
                        pltpu.make_async_copy(src, dst, w_rs.at[m, x]).start()

                @pl.when(jnp.logical_not(own))
                def _():
                    copy = remote(src, dst, w_ss.at[m, 2 * l + h], w_rs.at[m, x], dev(y, tx, z, h))
                    copy.start() if act == "start" else copy.wait_send()

    weights_x(0, w1_in, w1, "start")

    def swap_blocks(src, dst, cols, ss, rs, act):
        mine = part(z * 4 + x, CAP)
        for dz in ORDER:
            for dx in ORDER:
                i = dz * 4 + dx
                tx, tz = (x + dx) % 4, (z + dz) % 4
                theirs = part(tz * 4 + tx, CAP)
                if i == 0:
                    if act == "start":
                        pltpu.make_async_copy(src.at[mine, cols], dst.at[mine, cols], rs.at[0]).start()
                else:
                    copy = remote(
                        src.at[theirs, cols], dst.at[mine, cols], ss.at[i], rs.at[i], dev(y, tx, tz, c)
                    )
                    copy.start() if act == "start" else copy.wait_send()

    def swap_wait(dst, cols, rs, dz):
        for dx in range(4):
            block = ((z + 4 - dz) % 4) * 4 + (x + 4 - dx) % 4
            arrived(dst.at[part(block, CAP), cols], rs.at[dz * 4 + dx])

    lane = lax.broadcasted_iota(jnp.int32, (TOK, TOK), 1)
    sub = lax.broadcasted_iota(jnp.int32, (TOK, TOK), 0)

    def column(row):
        wide_row = jnp.broadcast_to(row.astype(F32), (TOK, TOK))
        return jnp.sum(jnp.where(lane == sub, wide_row, 0.0), axis=1, keepdims=True)

    seg_row = jnp.broadcast_to(seg[...].astype(F32), (TOK, TOK))
    seg_col = column(seg[...])
    earlier = jnp.sum((seg_row < seg_col).astype(F32), axis=1, keepdims=True)
    images = keep.shape[1]
    image = lax.broadcasted_iota(jnp.int32, (TOK, images), 1).astype(F32)
    kept = jnp.broadcast_to(keep[...].astype(F32), (TOK, images))
    keep_token = jnp.sum(jnp.where(image == seg_col, kept, 0.0), axis=1, keepdims=True)
    position = lax.broadcasted_iota(jnp.int32, (TOK, 1), 0).astype(F32)
    alive = (position - earlier < keep_token).astype(F32)
    acol[...] = alive
    expert = lax.broadcasted_iota(jnp.int32, (TOK, NE), 1).astype(F32)
    chosen = [column(ids[k : k + 1, :]) for k in range(2)]
    match = [(chosen[k] == expert).astype(F32) for k in range(2)]
    before = dot((lane < sub).astype(BF), (match[0] + match[1]).astype(BF), 1, 0)
    slot_iota = lax.broadcasted_iota(jnp.int32, (TOK, SLOTS), 1).astype(F32)
    for k in range(2):
        wcol[:, k : k + 1] = column(gw[k : k + 1, :]) * alive
        slot = jnp.sum(before * match[k], axis=1, keepdims=True)
        if k == 1:
            slot = slot + jnp.sum(match[0] * match[1], axis=1, keepdims=True)
        pt[k] = (slot_iota == chosen[k] * CAP + slot).astype(BF)

    every = pl.ds(0, D)
    wide = tok[...].astype(F32)
    centred = wide - jnp.mean(wide, axis=1, keepdims=True)
    scale = lax.rsqrt(jnp.mean(centred * centred, axis=1, keepdims=True) + epsilon)
    inv[...] = scale
    normed[...] = centred * scale
    feats = (normed[...].astype(BF).astype(F32) * alive).astype(BF)
    xs[...] = dot(pt[0] + pt[1], feats, 0, 0).astype(BF)
    swap_blocks(xs, x_all, every, a_ss.at[0], a_rs.at[0], "start")
    grads = [(cot[...].astype(F32) * wcol[:, k : k + 1]).astype(BF) for k in range(2)]
    gs[...] = (dot(pt[0], grads[0], 0, 0) + dot(pt[1], grads[1], 0, 0)).astype(BF)
    swap_blocks(gs, g_all, every, a_ss.at[1], a_rs.at[1], "start")
    weights_x(1, w2_in, w2, "start")

    own_rows, mate_rows = pl.ds(0, SLOTS), pl.ds(SLOTS, SLOTS)
    group = 4 * CAP

    def rows_y(k, ref, g):
        src = ref.at[part(g, group)]
        dst = ref.at[part(g + SLOTS // group, group)]
        return remote(src, dst, b_ss.at[k, g], b_rs.at[k, g], row_dev)

    def rows_on(k, ref):
        for dz in ORDER:
            swap_wait(ref, every, a_rs.at[k], dz)
            rows_y(k, ref, (z + 4 - dz) % 4).start()

    def piece(w, s, h, i):
        return w.at[part((2 * s + h) * 4 + i, HS)]

    def weights_y(m, w, i):
        return remote(piece(w, 0, 0, i), piece(w, 1, 0, i), wy_ss.at[m, i], wy_rs.at[m, i], wgt_dev)

    def weights_core(m, w, s, i):
        return remote(piece(w, s, 0, i), piece(w, s, 1, i), wc_ss.at[m, s, i], wc_rs.at[m, s, i], core_dev)

    def weights_mid(m, w):
        for dx in ORDER:
            i = (x + dx) % 4
            arrived(w.at[part(i, HS)], w_rs.at[m, i])
            weights_y(m, w, i).start()
            weights_core(m, w, 0, i).start()

    def weights_last(m, w):
        for dx in ORDER:
            i = (x + dx) % 4
            weights_y(m, w, i).wait_recv()
            weights_core(m, w, 1, i).start()

    def weights_here(m, w):
        for s in range(2):
            for i in range(4):
                weights_core(m, w, s, i).wait_recv()

    weights_mid(0, w1)
    rows_on(0, x_all)
    weights_mid(1, w2)
    rows_on(1, g_all)
    weights_last(0, w1)
    for g in range(4):
        rows_y(0, x_all, g).wait_recv()
    weights_here(0, w1)

    def tile(j, n=256):
        return pl.ds(pl.multiple_of(j * n, n), n)

    @pl.loop(0, HID // 256)
    def _(j):
        pre = dot(x_all[...], w1[tile(j), :], 1, 1)
        cdf = 0.5 * (1.0 + lax.erf(pre * root_half))
        value = (pre * cdf).astype(BF)
        hid[:, tile(j)] = value
        trans[tile(j), :] = value.T
        slope[:, tile(j)] = cdf + pre * jnp.exp(-0.5 * pre * pre) * density_scale

    weights_last(1, w2)
    for g in range(4):
        rows_y(1, g_all, g).wait_recv()

    def grads_core(m, send, core, s, n):
        return remote(
            send.at[s, :, tile(n)], core.at[s, :, tile(n)], gc_ss.at[m, s, n], gc_rs.at[m, s, n], core_dev
        )

    def grads_y(m, wp, far, n):
        return remote(wp.at[:, tile(n)], far.at[:, tile(n)], gy_ss.at[m, n], gy_rs.at[m, n], wgt_dev)

    def grads_tile(m, right, own, send, core, s, n):
        sums = dot(trans[pl.ds(s * 2 * Q, 2 * Q), :], right[:, tile(n)], 1, 0)
        own[s, :, tile(n)] = sums[:Q]
        send[s, :, tile(n)] = sums[Q:].astype(BF)
        grads_core(m, send, core, s, n).start()

    def weight_grads(m, right, own, send, core, wp, far):
        @pl.loop(0, D // 256)
        def _(n):
            grads_tile(m, right, own, send, core, 1, n)

        @pl.loop(0, D // 256)
        def _(n):
            grads_core(m, send, core, 1, n).wait_recv()
            wp[:, tile(n)] = (own[1, :, tile(n)] + core[1, :, tile(n)].astype(F32)).astype(BF)
            grads_y(m, wp, far, n).start()
            grads_tile(m, right, own, send, core, 0, n)

    def grads_x(m, fin, result, n, act):
        for i in range(4):
            src = fin.at[pl.ds(i * HS, HS), tile(n)]
            dst = result.at[x % 2, part(c, HS), tile(n)]
            rs = gx_rs.at[m, n, 2 * (x % 2) + c]
            own = jnp.logical_and(i == x, c == x // 2)

            @pl.when(own)
            def _():
                if act == "start":
                    pltpu.make_async_copy(src, dst, rs).start()

            @pl.when(jnp.logical_not(own))
            def _():
                copy = remote(src, dst, gx_ss.at[m, n, i], rs, dev(y, i, z, x // 2))
                copy.start() if act == "start" else copy.wait_send()

    def grads_last(m, own, send, core, wp, far, fin, result):
        @pl.loop(0, D // 256)
        def _(n):
            grads_core(m, send, core, 0, n).wait_recv()
            grads_y(m, wp, far, n).wait_recv()
            sums = own[0, :, tile(n)] + core[0, :, tile(n)].astype(F32) + far[:, tile(n)].astype(F32)
            fin[:, tile(n)] = sums.astype(BF)
            grads_x(m, fin, result, n, "start")

    def sums_y(k, send, recv, n):
        return remote(send.at[:, tile(n)], recv.at[:, tile(n)], p_ss.at[k, n], p_rs.at[k, n], row_dev)

    def results_mate(k, left, w, send, recv):
        @pl.loop(0, D // 256)
        def _(n):
            send[:, tile(n)] = dot(left[mate_rows, :], w[:, tile(n)], 1, 0).astype(BF)
            sums_y(k, send, recv, n).start()

    def results_own(k, left, w, send, recv, fin, ret):
        for h, (low, high) in enumerate(SPANS):

            @pl.loop(low, high)
            def _(n):
                own = dot(left[own_rows, :], w[:, tile(n)], 1, 0)
                sums_y(k, send, recv, n).wait_recv()
                fin[:, tile(n)] = (own + recv[:, tile(n)].astype(F32)).astype(BF)

            swap_blocks(fin, ret, span(h), q_ss.at[k, h], q_rs.at[k, h], "start")

    def span(h):
        return pl.ds(SPANS[h][0] * 256, (SPANS[h][1] - SPANS[h][0]) * 256)

    weight_grads(1, g_all, r_own, r_send, r_core, r_wp, r_far)
    weights_here(1, w2)
    results_mate(0, hid, w2, y_send, y_recv)

    @pl.loop(0, HID // 256)
    def _(j):
        back = dot(g_all[...], w2[tile(j), :], 1, 1)
        value = (back * slope[:, tile(j)]).astype(BF)
        dpre[:, tile(j)] = value
        trans[tile(j), :] = value.T

    results_mate(1, dpre, w1, d_send, d_recv)
    weight_grads(0, x_all, e_own, e_send, e_core, e_wp, e_far)
    results_own(0, hid, w2, y_send, y_recv, y_fin, y_ret)
    grads_last(1, r_own, r_send, r_core, r_wp, r_far, r_fin, rg)
    results_own(1, dpre, w1, d_send, d_recv, d_fin, d_ret)

    for h in range(len(SPANS)):
        for dz in range(4):
            swap_wait(y_ret, span(h), q_rs.at[0, h], dz)
    result = tok[...].astype(F32)
    for k in range(2):
        pick = dot(pt[k], y_ret[...], 1, 0)
        result = result + pick * wcol[:, k : k + 1]
        inner = acol[...] * jnp.sum(cot[...].astype(F32) * pick, axis=1, keepdims=True)
        gg[k : k + 1, :] = jnp.sum(jnp.where(lane == sub, inner, 0.0), axis=0, keepdims=True)
    out[...] = result.astype(BF)
    for h in range(len(SPANS)):
        for dz in range(4):
            swap_wait(d_ret, span(h), q_rs.at[1, h], dz)
    dnorm = (dot(pt[0], d_ret[...], 1, 0) + dot(pt[1], d_ret[...], 1, 0)) * acol[...]
    tail = dnorm - jnp.mean(dnorm, axis=1, keepdims=True)
    tail = tail - normed[...] * jnp.mean(dnorm * normed[...], axis=1, keepdims=True)
    tg[...] = (cot[...].astype(F32) + inv[...] * tail).astype(BF)

    grads_last(0, e_own, e_send, e_core, e_wp, e_far, e_fin, eg)

    for m, result in ((1, rg), (0, eg)):

        @pl.loop(0, D // 256)
        def _(n):
            for l in range(2):
                for h in range(2):
                    arrived(result.at[l, pl.ds(h * HS, HS), tile(n)], gx_rs.at[m, n, 2 * l + h])

    for m, (w_in, w) in enumerate(((w1_in, w1), (w2_in, w2))):
        weights_x(m, w_in, w, "wait")
        for i in range(4):
            weights_y(m, w, i).wait_send()
            for s in range(2):
                weights_core(m, w, s, i).wait_send()
    for k, (src, dst) in enumerate(((xs, x_all), (gs, g_all))):
        swap_blocks(src, dst, every, a_ss.at[k], a_rs.at[k], "wait")
        for g in range(4):
            rows_y(k, dst, g).wait_send()
    for k, (send, recv, fin, ret) in enumerate(((y_send, y_recv, y_fin, y_ret), (d_send, d_recv, d_fin, d_ret))):
        for h in range(len(SPANS)):
            swap_blocks(fin, ret, span(h), q_ss.at[k, h], q_rs.at[k, h], "wait")

        @pl.loop(0, D // 256)
        def _(n):
            sums_y(k, send, recv, n).wait_send()

    for m, send, core, wp, far, fin, result in (
        (0, e_send, e_core, e_wp, e_far, e_fin, eg),
        (1, r_send, r_core, r_wp, r_far, r_fin, rg),
    ):

        @pl.loop(0, D // 256)
        def _(n):
            for s in range(2):
                grads_core(m, send, core, s, n).wait_send()
            grads_y(m, wp, far, n).wait_send()
            grads_x(m, fin, result, n, "wait")


def hand_out(*refs):
    sems = refs[-1]
    half = len(refs) // 2
    copies = [pltpu.make_async_copy(refs[i], refs[half + i], sems.at[i]) for i in range(half)]
    for copy in copies:
        copy.start()
    for copy in copies:
        copy.wait()


def body(tokens, cotangent, gate_weights, expert_ids, *rest):
    vmem = pl.BlockSpec(memory_space=pltpu.VMEM)
    hbm = pl.BlockSpec(memory_space=pl.ANY)
    dma = pltpu.SemaphoreType.DMA
    shape = jax.ShapeDtypeStruct
    tiles = D // 256
    grad_scratch = [
        pltpu.VMEM((2, Q, D), F32),
        pltpu.VMEM((2, Q, D), BF),
        pltpu.VMEM((2, Q, D), BF),
        pltpu.VMEM((Q, D), BF),
        pltpu.VMEM((Q, D), BF),
        pltpu.VMEM((Q, D), BF),
    ]
    shapes = (
        shape((TOK, D), BF),
        shape((TOK, D), BF),
        shape((2, TOK), F32),
        shape((2, SH, D), BF),
        shape((2, SH, D), BF),
    )
    results = pl.pallas_call(
        kernel,
        out_shape=shapes,
        in_specs=[vmem] * 6 + [hbm] * 2,
        out_specs=(vmem, vmem, vmem, hbm, hbm),
        scratch_shapes=[
            pltpu.VMEM((2, TOK, SLOTS), BF),
            pltpu.VMEM((TOK, D), F32),
            pltpu.VMEM((TOK, 1), F32),
            pltpu.VMEM((TOK, 2), F32),
            pltpu.VMEM((TOK, 1), F32),
            pltpu.VMEM((SLOTS, D), BF),
            pltpu.VMEM((SLOTS, D), BF),
            pltpu.VMEM((ROWS, D), BF),
            pltpu.VMEM((ROWS, D), BF),
            pltpu.VMEM((HID, D), BF),
            pltpu.VMEM((HID, D), BF),
            pltpu.VMEM((ROWS, HID), BF),
            pltpu.VMEM((ROWS, HID), F32),
            pltpu.VMEM((ROWS, HID), BF),
            pltpu.VMEM((HID, ROWS), BF),
        ]
        + [pltpu.VMEM((SLOTS, D), BF)] * 8
        + grad_scratch * 2
        + [
            dma((2, NE)),
            dma((2, NE)),
            dma((2, 4)),
            dma((2, 4)),
            dma((2, tiles)),
            dma((2, tiles)),
            dma((2, len(SPANS), NE)),
            dma((2, len(SPANS), NE)),
            dma((2, 4)),
            dma((2, 4)),
            dma((2, 4)),
            dma((2, 4)),
            dma((2, 2, 4)),
            dma((2, 2, 4)),
            dma((2, 2, tiles)),
            dma((2, 2, tiles)),
            dma((2, tiles)),
            dma((2, tiles)),
            dma((2, tiles, 4)),
            dma((2, tiles, 4)),
        ],
        compiler_params=pltpu.CompilerParams(
            collective_id=0, has_side_effects=True, vmem_limit_bytes=60 * 2**20
        ),
    )(tokens, cotangent, gate_weights.T, expert_ids.T, *rest)
    out, tg, gg, eg, rg = pl.pallas_call(
        hand_out,
        out_shape=shapes,
        in_specs=[hbm] * 5,
        out_specs=(hbm,) * 5,
        scratch_shapes=[dma((5,))],
    )(*results)
    return out, tg, gg.T, eg, rg


def solution(mesh):
    rows = P(("dp", "expert"), None)
    weights = P("expert", "dp", None)
    return jax.shard_map(
        body,
        mesh=mesh,
        in_specs=(rows,) * 6 + (weights,) * 2,
        out_specs=(rows,) * 3 + (weights,) * 2,
        check_vma=False,
    )
```

```python
import jax
import jax.numpy as jnp
from jax import lax
from jax.experimental import pallas as pl
from jax.experimental.pallas import tpu as pltpu
from jax.sharding import PartitionSpec as P

MESH = pl.DeviceIdType.MESH
epsilon = 1e-06
root_half = 0.7071067811865476
density_scale = 0.3989422804014327

D = 1280
TOK = 128
SLOTS = 256
CAP = 16
NE = 16
SH = 160
HS = SH // 2
Q = 4 * HS
HID = 4 * Q
ROWS = 2 * SLOTS
ORDER = (0, 1, 3, 2)
SPANS = ((0, 3), (3, 5))
BF = jnp.bfloat16
F32 = jnp.float32


def dot(a, b, ca, cb):
    return lax.dot_general(a, b, (((ca,), (cb,)), ((), ())), preferred_element_type=F32)


def kernel(
    tok, cot, gw, ids, seg, keep, w1_in, w2_in,
    out, tg, gg, eg, rg,
    pt, normed, inv, wcol, acol, xs, gs, x_all, g_all, w1, w2, hid, slope, dpre, trans,
    y_send, y_recv, y_fin, y_ret, d_send, d_recv, d_fin, d_ret,
    e_own, e_send, e_core, e_wp, e_far, e_fin, r_own, r_send, r_core, r_wp, r_far, r_fin,
    a_ss, a_rs, b_ss, b_rs, p_ss, p_rs, q_ss, q_rs, w_ss, w_rs, wy_ss, wy_rs, wc_ss, wc_rs,
    gc_ss, gc_rs, gy_ss, gy_rs, gx_ss, gx_rs,
):
    dp = lax.axis_index("dp")
    ex = lax.axis_index("expert")
    y, x = dp // 4, dp % 4
    z, c = ex // 2, ex % 2
    row_mate = y + 1 - 2 * (y % 2)
    wgt_mate = (y + 5 - 2 * ((y + 1) % 2)) % 4
    other = 1 - c

    def dev(yy, xx, zz, cc):
        return (yy * 4 + xx, zz * 2 + cc)

    row_dev = dev(row_mate, x, z, c)
    wgt_dev = dev(wgt_mate, x, z, c)
    core_dev = dev(y, x, z, other)

    def remote(src, dst, ss, rs, target):
        return pltpu.make_async_remote_copy(
            src_ref=src, dst_ref=dst, send_sem=ss, recv_sem=rs, device_id=target, device_id_type=MESH
        )

    def arrived(dst, rs):
        pltpu.make_async_copy(dst, dst, rs).wait()

    def part(i, n):
        return pl.ds(pl.multiple_of(i * n, n), n)

    barrier = pltpu.get_barrier_semaphore()
    for dz in range(4):
        for dx in range(4):
            if dz or dx:
                pl.semaphore_signal(
                    barrier, inc=1, device_id=dev(y, (x + dx) % 4, (z + dz) % 4, c), device_id_type=MESH
                )
    for i in range(4):
        pl.semaphore_signal(barrier, inc=1, device_id=dev(y, i, z, other), device_id_type=MESH)
    for target in (row_dev, wgt_dev):
        pl.semaphore_signal(barrier, inc=1, device_id=target, device_id_type=MESH)

    def weights_x(m, w_in, w, act):
        for l in range(2):
            for h in range(2):
                tx = 2 * c + l
                src = w_in.at[l, pl.ds(HS * h, HS)]
                dst = w.at[part(x, HS)]
                own = jnp.logical_and(tx == x, h == c)

                @pl.when(own)
                def _():
                    if act == "start":
                        pltpu.make_async_copy(src, dst, w_rs.at[m, x]).start()

                @pl.when(jnp.logical_not(own))
                def _():
                    copy = remote(src, dst, w_ss.at[m, 2 * l + h], w_rs.at[m, x], dev(y, tx, z, h))
                    copy.start() if act == "start" else copy.wait_send()

    def swap_blocks(src, dst, cols, ss, rs, act):
        mine = part(z * 4 + x, CAP)
        for dz in ORDER:
            for dx in ORDER:
                i = dz * 4 + dx
                tx, tz = (x + dx) % 4, (z + dz) % 4
                theirs = part(tz * 4 + tx, CAP)
                if i == 0:
                    if act == "start":
                        pltpu.make_async_copy(src.at[mine, cols], dst.at[mine, cols], rs.at[0]).start()
                else:
                    copy = remote(
                        src.at[theirs, cols], dst.at[mine, cols], ss.at[i], rs.at[i], dev(y, tx, tz, c)
                    )
                    copy.start() if act == "start" else copy.wait_send()

    def swap_wait(dst, cols, rs, dz):
        for dx in range(4):
            block = ((z + 4 - dz) % 4) * 4 + (x + 4 - dx) % 4
            arrived(dst.at[part(block, CAP), cols], rs.at[dz * 4 + dx])

    lane = lax.broadcasted_iota(jnp.int32, (TOK, TOK), 1)
    sub = lax.broadcasted_iota(jnp.int32, (TOK, TOK), 0)

    def column(row):
        wide_row = jnp.broadcast_to(row.astype(F32), (TOK, TOK))
        return jnp.sum(jnp.where(lane == sub, wide_row, 0.0), axis=1, keepdims=True)

    seg_row = jnp.broadcast_to(seg[...].astype(F32), (TOK, TOK))
    seg_col = column(seg[...])
    earlier = jnp.sum((seg_row < seg_col).astype(F32), axis=1, keepdims=True)
    images = keep.shape[1]
    image = lax.broadcasted_iota(jnp.int32, (TOK, images), 1).astype(F32)
    kept = jnp.broadcast_to(keep[...].astype(F32), (TOK, images))
    keep_token = jnp.sum(jnp.where(image == seg_col, kept, 0.0), axis=1, keepdims=True)
    position = lax.broadcasted_iota(jnp.int32, (TOK, 1), 0).astype(F32)
    alive = (position - earlier < keep_token).astype(F32)
    acol[...] = alive
    expert = lax.broadcasted_iota(jnp.int32, (TOK, NE), 1).astype(F32)
    chosen = [column(ids[k : k + 1, :]) for k in range(2)]
    match = [(chosen[k] == expert).astype(F32) for k in range(2)]
    before = dot((lane < sub).astype(BF), (match[0] + match[1]).astype(BF), 1, 0)
    slot_iota = lax.broadcasted_iota(jnp.int32, (TOK, SLOTS), 1).astype(F32)
    for k in range(2):
        wcol[:, k : k + 1] = column(gw[k : k + 1, :]) * alive
        slot = jnp.sum(before * match[k], axis=1, keepdims=True)
        if k == 1:
            slot = slot + jnp.sum(match[0] * match[1], axis=1, keepdims=True)
        pt[k] = (slot_iota == chosen[k] * CAP + slot).astype(BF)

    every = pl.ds(0, D)
    wide = tok[...].astype(F32)
    centred = wide - jnp.mean(wide, axis=1, keepdims=True)
    scale = lax.rsqrt(jnp.mean(centred * centred, axis=1, keepdims=True) + epsilon)
    inv[...] = scale
    normed[...] = centred * scale
    feats = (normed[...].astype(BF).astype(F32) * alive).astype(BF)
    xs[...] = dot(pt[0] + pt[1], feats, 0, 0).astype(BF)

    pl.semaphore_wait(barrier, NE - 1 + 4 + 2)
    weights_x(0, w1_in, w1, "start")
    swap_blocks(xs, x_all, every, a_ss.at[0], a_rs.at[0], "start")
    grads = [(cot[...].astype(F32) * wcol[:, k : k + 1]).astype(BF) for k in range(2)]
    gs[...] = (dot(pt[0], grads[0], 0, 0) + dot(pt[1], grads[1], 0, 0)).astype(BF)
    swap_blocks(gs, g_all, every, a_ss.at[1], a_rs.at[1], "start")
    weights_x(1, w2_in, w2, "start")

    own_rows, mate_rows = pl.ds(0, SLOTS), pl.ds(SLOTS, SLOTS)
    group = 4 * CAP

    def rows_y(k, ref, g):
        src = ref.at[part(g, group)]
        dst = ref.at[part(g + SLOTS // group, group)]
        return remote(src, dst, b_ss.at[k, g], b_rs.at[k, g], row_dev)

    def rows_on(k, ref):
        for dz in ORDER:
            swap_wait(ref, every, a_rs.at[k], dz)
            rows_y(k, ref, (z + 4 - dz) % 4).start()

    def piece(w, s, h, i):
        return w.at[part((2 * s + h) * 4 + i, HS)]

    def weights_y(m, w, i):
        return remote(piece(w, 0, 0, i), piece(w, 1, 0, i), wy_ss.at[m, i], wy_rs.at[m, i], wgt_dev)

    def weights_core(m, w, s, i):
        return remote(piece(w, s, 0, i), piece(w, s, 1, i), wc_ss.at[m, s, i], wc_rs.at[m, s, i], core_dev)

    def weights_mid(m, w):
        for dx in ORDER:
            i = (x + dx) % 4
            arrived(w.at[part(i, HS)], w_rs.at[m, i])
            weights_y(m, w, i).start()
            weights_core(m, w, 0, i).start()

    def weights_last(m, w):
        for dx in ORDER:
            i = (x + dx) % 4
            weights_y(m, w, i).wait_recv()
            weights_core(m, w, 1, i).start()

    def weights_here(m, w):
        for s in range(2):
            for i in range(4):
                weights_core(m, w, s, i).wait_recv()

    weights_mid(0, w1)
    rows_on(0, x_all)
    weights_mid(1, w2)
    rows_on(1, g_all)
    weights_last(0, w1)
    for g in range(4):
        rows_y(0, x_all, g).wait_recv()
    weights_here(0, w1)

    def tile(j, n=256):
        return pl.ds(pl.multiple_of(j * n, n), n)

    @pl.loop(0, HID // 256)
    def _(j):
        pre = dot(x_all[...], w1[tile(j), :], 1, 1)
        cdf = 0.5 * (1.0 + lax.erf(pre * root_half))
        value = (pre * cdf).astype(BF)
        hid[:, tile(j)] = value
        trans[tile(j), :] = value.T
        slope[:, tile(j)] = cdf + pre * jnp.exp(-0.5 * pre * pre) * density_scale

    weights_last(1, w2)
    for g in range(4):
        rows_y(1, g_all, g).wait_recv()

    def grads_core(m, send, core, s, n):
        return remote(
            send.at[s, :, tile(n)], core.at[s, :, tile(n)], gc_ss.at[m, s, n], gc_rs.at[m, s, n], core_dev
        )

    def grads_y(m, wp, far, n):
        return remote(wp.at[:, tile(n)], far.at[:, tile(n)], gy_ss.at[m, n], gy_rs.at[m, n], wgt_dev)

    def grads_tile(m, right, own, send, core, s, n):
        sums = dot(trans[pl.ds(s * 2 * Q, 2 * Q), :], right[:, tile(n)], 1, 0)
        own[s, :, tile(n)] = sums[:Q]
        send[s, :, tile(n)] = sums[Q:].astype(BF)
        grads_core(m, send, core, s, n).start()

    def weight_grads(m, right, own, send, core, wp, far):
        @pl.loop(0, D // 256)
        def _(n):
            grads_tile(m, right, own, send, core, 1, n)

        @pl.loop(0, D // 256)
        def _(n):
            grads_core(m, send, core, 1, n).wait_recv()
            wp[:, tile(n)] = (own[1, :, tile(n)] + core[1, :, tile(n)].astype(F32)).astype(BF)
            grads_y(m, wp, far, n).start()
            grads_tile(m, right, own, send, core, 0, n)

    def grads_x(m, fin, result, n, act):
        for i in range(4):
            src = fin.at[pl.ds(i * HS, HS), tile(n)]
            dst = result.at[x % 2, part(c, HS), tile(n)]
            rs = gx_rs.at[m, n, 2 * (x % 2) + c]
            own = jnp.logical_and(i == x, c == x // 2)

            @pl.when(own)
            def _():
                if act == "start":
                    pltpu.make_async_copy(src, dst, rs).start()

            @pl.when(jnp.logical_not(own))
            def _():
                copy = remote(src, dst, gx_ss.at[m, n, i], rs, dev(y, i, z, x // 2))
                copy.start() if act == "start" else copy.wait_send()

    def grads_last(m, own, send, core, wp, far, fin, result):
        @pl.loop(0, D // 256)
        def _(n):
            grads_core(m, send, core, 0, n).wait_recv()
            grads_y(m, wp, far, n).wait_recv()
            sums = own[0, :, tile(n)] + core[0, :, tile(n)].astype(F32) + far[:, tile(n)].astype(F32)
            fin[:, tile(n)] = sums.astype(BF)
            grads_x(m, fin, result, n, "start")

    def sums_y(k, send, recv, n):
        return remote(send.at[:, tile(n)], recv.at[:, tile(n)], p_ss.at[k, n], p_rs.at[k, n], row_dev)

    def results_mate(k, left, w, send, recv):
        @pl.loop(0, D // 256)
        def _(n):
            send[:, tile(n)] = dot(left[mate_rows, :], w[:, tile(n)], 1, 0).astype(BF)
            sums_y(k, send, recv, n).start()

    def results_own(k, left, w, send, recv, fin, ret):
        for h, (low, high) in enumerate(SPANS):

            @pl.loop(low, high)
            def _(n):
                own = dot(left[own_rows, :], w[:, tile(n)], 1, 0)
                sums_y(k, send, recv, n).wait_recv()
                fin[:, tile(n)] = (own + recv[:, tile(n)].astype(F32)).astype(BF)

            swap_blocks(fin, ret, span(h), q_ss.at[k, h], q_rs.at[k, h], "start")

    def span(h):
        return pl.ds(SPANS[h][0] * 256, (SPANS[h][1] - SPANS[h][0]) * 256)

    weight_grads(1, g_all, r_own, r_send, r_core, r_wp, r_far)
    weights_here(1, w2)
    results_mate(0, hid, w2, y_send, y_recv)

    @pl.loop(0, HID // 256)
    def _(j):
        back = dot(g_all[...], w2[tile(j), :], 1, 1)
        value = (back * slope[:, tile(j)]).astype(BF)
        dpre[:, tile(j)] = value
        trans[tile(j), :] = value.T

    results_mate(1, dpre, w1, d_send, d_recv)
    weight_grads(0, x_all, e_own, e_send, e_core, e_wp, e_far)
    results_own(0, hid, w2, y_send, y_recv, y_fin, y_ret)
    grads_last(1, r_own, r_send, r_core, r_wp, r_far, r_fin, rg)
    results_own(1, dpre, w1, d_send, d_recv, d_fin, d_ret)

    for h in range(len(SPANS)):
        for dz in range(4):
            swap_wait(y_ret, span(h), q_rs.at[0, h], dz)
    result = tok[...].astype(F32)
    for k in range(2):
        pick = dot(pt[k], y_ret[...], 1, 0)
        result = result + pick * wcol[:, k : k + 1]
        inner = acol[...] * jnp.sum(cot[...].astype(F32) * pick, axis=1, keepdims=True)
        gg[k : k + 1, :] = jnp.sum(jnp.where(lane == sub, inner, 0.0), axis=0, keepdims=True)
    out[...] = result.astype(BF)
    for h in range(len(SPANS)):
        for dz in range(4):
            swap_wait(d_ret, span(h), q_rs.at[1, h], dz)
    dnorm = (dot(pt[0], d_ret[...], 1, 0) + dot(pt[1], d_ret[...], 1, 0)) * acol[...]
    tail = dnorm - jnp.mean(dnorm, axis=1, keepdims=True)
    tail = tail - normed[...] * jnp.mean(dnorm * normed[...], axis=1, keepdims=True)
    tg[...] = (cot[...].astype(F32) + inv[...] * tail).astype(BF)

    grads_last(0, e_own, e_send, e_core, e_wp, e_far, e_fin, eg)

    for m, result in ((1, rg), (0, eg)):

        @pl.loop(0, D // 256)
        def _(n):
            for l in range(2):
                for h in range(2):
                    arrived(result.at[l, pl.ds(h * HS, HS), tile(n)], gx_rs.at[m, n, 2 * l + h])

    for m, (w_in, w) in enumerate(((w1_in, w1), (w2_in, w2))):
        weights_x(m, w_in, w, "wait")
        for i in range(4):
            weights_y(m, w, i).wait_send()
            for s in range(2):
                weights_core(m, w, s, i).wait_send()
    for k, (src, dst) in enumerate(((xs, x_all), (gs, g_all))):
        swap_blocks(src, dst, every, a_ss.at[k], a_rs.at[k], "wait")
        for g in range(4):
            rows_y(k, dst, g).wait_send()
    for k, (send, recv, fin, ret) in enumerate(((y_send, y_recv, y_fin, y_ret), (d_send, d_recv, d_fin, d_ret))):
        for h in range(len(SPANS)):
            swap_blocks(fin, ret, span(h), q_ss.at[k, h], q_rs.at[k, h], "wait")

        @pl.loop(0, D // 256)
        def _(n):
            sums_y(k, send, recv, n).wait_send()

    for m, send, core, wp, far, fin, result in (
        (0, e_send, e_core, e_wp, e_far, e_fin, eg),
        (1, r_send, r_core, r_wp, r_far, r_fin, rg),
    ):

        @pl.loop(0, D // 256)
        def _(n):
            for s in range(2):
                grads_core(m, send, core, s, n).wait_send()
            grads_y(m, wp, far, n).wait_send()
            grads_x(m, fin, result, n, "wait")


def hand_out(*refs):
    sems = refs[-1]
    half = len(refs) // 2
    copies = [pltpu.make_async_copy(refs[i], refs[half + i], sems.at[i]) for i in range(half)]
    for copy in copies:
        copy.start()
    for copy in copies:
        copy.wait()


def body(tokens, cotangent, gate_weights, expert_ids, *rest):
    vmem = pl.BlockSpec(memory_space=pltpu.VMEM)
    hbm = pl.BlockSpec(memory_space=pl.ANY)
    dma = pltpu.SemaphoreType.DMA
    shape = jax.ShapeDtypeStruct
    tiles = D // 256
    grad_scratch = [
        pltpu.VMEM((2, Q, D), F32),
        pltpu.VMEM((2, Q, D), BF),
        pltpu.VMEM((2, Q, D), BF),
        pltpu.VMEM((Q, D), BF),
        pltpu.VMEM((Q, D), BF),
        pltpu.VMEM((Q, D), BF),
    ]
    shapes = (
        shape((TOK, D), BF),
        shape((TOK, D), BF),
        shape((2, TOK), F32),
        shape((2, SH, D), BF),
        shape((2, SH, D), BF),
    )
    results = pl.pallas_call(
        kernel,
        out_shape=shapes,
        in_specs=[vmem] * 6 + [hbm] * 2,
        out_specs=(vmem, vmem, vmem, hbm, hbm),
        scratch_shapes=[
            pltpu.VMEM((2, TOK, SLOTS), BF),
            pltpu.VMEM((TOK, D), F32),
            pltpu.VMEM((TOK, 1), F32),
            pltpu.VMEM((TOK, 2), F32),
            pltpu.VMEM((TOK, 1), F32),
            pltpu.VMEM((SLOTS, D), BF),
            pltpu.VMEM((SLOTS, D), BF),
            pltpu.VMEM((ROWS, D), BF),
            pltpu.VMEM((ROWS, D), BF),
            pltpu.VMEM((HID, D), BF),
            pltpu.VMEM((HID, D), BF),
            pltpu.VMEM((ROWS, HID), BF),
            pltpu.VMEM((ROWS, HID), F32),
            pltpu.VMEM((ROWS, HID), BF),
            pltpu.VMEM((HID, ROWS), BF),
        ]
        + [pltpu.VMEM((SLOTS, D), BF)] * 8
        + grad_scratch * 2
        + [
            dma((2, NE)),
            dma((2, NE)),
            dma((2, 4)),
            dma((2, 4)),
            dma((2, tiles)),
            dma((2, tiles)),
            dma((2, len(SPANS), NE)),
            dma((2, len(SPANS), NE)),
            dma((2, 4)),
            dma((2, 4)),
            dma((2, 4)),
            dma((2, 4)),
            dma((2, 2, 4)),
            dma((2, 2, 4)),
            dma((2, 2, tiles)),
            dma((2, 2, tiles)),
            dma((2, tiles)),
            dma((2, tiles)),
            dma((2, tiles, 4)),
            dma((2, tiles, 4)),
        ],
        compiler_params=pltpu.CompilerParams(
            collective_id=0, has_side_effects=True, vmem_limit_bytes=60 * 2**20
        ),
    )(tokens, cotangent, gate_weights.T, expert_ids.T, *rest)
    out, tg, gg, eg, rg = pl.pallas_call(
        hand_out,
        out_shape=shapes,
        in_specs=[hbm] * 5,
        out_specs=(vmem,) * 5,
        scratch_shapes=[dma((5,))],
    )(*results)
    return out, tg, gg.T, eg, rg


def solution(mesh):
    rows = P(("dp", "expert"), None)
    weights = P("expert", "dp", None)
    return jax.shard_map(
        body,
        mesh=mesh,
        in_specs=(rows,) * 6 + (weights,) * 2,
        out_specs=(rows,) * 3 + (weights,) * 2,
        check_vma=False,
    )
```

```python
import jax
import jax.numpy as jnp
from jax import lax
from jax.experimental import pallas as pl
from jax.experimental.pallas import tpu as pltpu
from jax.sharding import PartitionSpec as P

MESH = pl.DeviceIdType.MESH
epsilon = 1e-06
root_half = 0.7071067811865476
density_scale = 0.3989422804014327

D = 1280
TOK = 128
SLOTS = 256
CAP = 16
NE = 16
SH = 160
HS = SH // 2
Q = 4 * HS
HID = 4 * Q
ROWS = 2 * SLOTS
ORDER = (0, 1, 3, 2)
SPANS = ((0, 3), (3, 5))
BF = jnp.bfloat16
F32 = jnp.float32


def dot(a, b, ca, cb):
    return lax.dot_general(a, b, (((ca,), (cb,)), ((), ())), preferred_element_type=F32)


def kernel(
    tok, cot, gw, ids, seg, keep, w1_in, w2_in,
    out, tg, gg, eg, rg,
    pt, normed, inv, wcol, acol, xs, gs, x_all, g_all, w1, w2, hid, slope, dpre, trans,
    y_send, y_recv, y_fin, y_ret, d_send, d_recv, d_fin, d_ret,
    e_own, e_send, e_core, e_wp, e_far, e_fin, r_own, r_send, r_core, r_wp, r_far, r_fin,
    a_ss, a_rs, b_ss, b_rs, p_ss, p_rs, q_ss, q_rs, w_ss, w_rs, wy_ss, wy_rs, wc_ss, wc_rs,
    gc_ss, gc_rs, gy_ss, gy_rs, gx_ss, gx_rs,
):
    dp = lax.axis_index("dp")
    ex = lax.axis_index("expert")
    y, x = dp // 4, dp % 4
    z, c = ex // 2, ex % 2
    row_mate = y + 1 - 2 * (y % 2)
    wgt_mate = (y + 5 - 2 * ((y + 1) % 2)) % 4
    other = 1 - c

    def dev(yy, xx, zz, cc):
        return (yy * 4 + xx, zz * 2 + cc)

    row_dev = dev(row_mate, x, z, c)
    wgt_dev = dev(wgt_mate, x, z, c)
    core_dev = dev(y, x, z, other)

    def remote(src, dst, ss, rs, target):
        return pltpu.make_async_remote_copy(
            src_ref=src, dst_ref=dst, send_sem=ss, recv_sem=rs, device_id=target, device_id_type=MESH
        )

    def arrived(dst, rs):
        pltpu.make_async_copy(dst, dst, rs).wait()

    def part(i, n):
        return pl.ds(pl.multiple_of(i * n, n), n)

    barrier = pltpu.get_barrier_semaphore()
    for dz in range(4):
        for dx in range(4):
            if dz or dx:
                pl.semaphore_signal(
                    barrier, inc=1, device_id=dev(y, (x + dx) % 4, (z + dz) % 4, c), device_id_type=MESH
                )
    for i in range(4):
        pl.semaphore_signal(barrier, inc=1, device_id=dev(y, i, z, other), device_id_type=MESH)
    for target in (row_dev, wgt_dev):
        pl.semaphore_signal(barrier, inc=1, device_id=target, device_id_type=MESH)

    def weights_x(m, w_in, w, act):
        for l in range(2):
            for h in range(2):
                tx = 2 * c + l
                src = w_in.at[l, pl.ds(HS * h, HS)]
                dst = w.at[part(x, HS)]
                own = jnp.logical_and(tx == x, h == c)

                @pl.when(own)
                def _():
                    if act == "start":
                        pltpu.make_async_copy(src, dst, w_rs.at[m, x]).start()

                @pl.when(jnp.logical_not(own))
                def _():
                    copy = remote(src, dst, w_ss.at[m, 2 * l + h], w_rs.at[m, x], dev(y, tx, z, h))
                    copy.start() if act == "start" else copy.wait_send()

    def swap_blocks(src, dst, cols, ss, rs, act):
        mine = part(z * 4 + x, CAP)
        for dz in ORDER:
            for dx in ORDER:
                i = dz * 4 + dx
                tx, tz = (x + dx) % 4, (z + dz) % 4
                theirs = part(tz * 4 + tx, CAP)
                if i == 0:
                    if act == "start":
                        pltpu.make_async_copy(src.at[mine, cols], dst.at[mine, cols], rs.at[0]).start()
                else:
                    copy = remote(
                        src.at[theirs, cols], dst.at[mine, cols], ss.at[i], rs.at[i], dev(y, tx, tz, c)
                    )
                    copy.start() if act == "start" else copy.wait_send()

    def swap_wait(dst, cols, rs, dz):
        for dx in range(4):
            block = ((z + 4 - dz) % 4) * 4 + (x + 4 - dx) % 4
            arrived(dst.at[part(block, CAP), cols], rs.at[dz * 4 + dx])

    lane = lax.broadcasted_iota(jnp.int32, (TOK, TOK), 1)
    sub = lax.broadcasted_iota(jnp.int32, (TOK, TOK), 0)

    def column(row):
        wide_row = jnp.broadcast_to(row.astype(F32), (TOK, TOK))
        return jnp.sum(jnp.where(lane == sub, wide_row, 0.0), axis=1, keepdims=True)

    seg_row = jnp.broadcast_to(seg[...].astype(F32), (TOK, TOK))
    seg_col = column(seg[...])
    earlier = jnp.sum((seg_row < seg_col).astype(F32), axis=1, keepdims=True)
    images = keep.shape[1]
    image = lax.broadcasted_iota(jnp.int32, (TOK, images), 1).astype(F32)
    kept = jnp.broadcast_to(keep[...].astype(F32), (TOK, images))
    keep_token = jnp.sum(jnp.where(image == seg_col, kept, 0.0), axis=1, keepdims=True)
    position = lax.broadcasted_iota(jnp.int32, (TOK, 1), 0).astype(F32)
    alive = (position - earlier < keep_token).astype(F32)
    acol[...] = alive
    expert = lax.broadcasted_iota(jnp.int32, (TOK, NE), 1).astype(F32)
    chosen = [column(ids[k : k + 1, :]) for k in range(2)]
    match = [(chosen[k] == expert).astype(F32) for k in range(2)]
    before = dot((lane < sub).astype(BF), (match[0] + match[1]).astype(BF), 1, 0)
    slot_iota = lax.broadcasted_iota(jnp.int32, (TOK, SLOTS), 1).astype(F32)
    for k in range(2):
        wcol[:, k : k + 1] = column(gw[k : k + 1, :]) * alive
        slot = jnp.sum(before * match[k], axis=1, keepdims=True)
        if k == 1:
            slot = slot + jnp.sum(match[0] * match[1], axis=1, keepdims=True)
        pt[k] = (slot_iota == chosen[k] * CAP + slot).astype(BF)

    every = pl.ds(0, D)
    wide = tok[...].astype(F32)
    centred = wide - jnp.mean(wide, axis=1, keepdims=True)
    scale = lax.rsqrt(jnp.mean(centred * centred, axis=1, keepdims=True) + epsilon)
    inv[...] = scale
    normed[...] = centred * scale
    feats = (normed[...].astype(BF).astype(F32) * alive).astype(BF)
    xs[...] = dot(pt[0] + pt[1], feats, 0, 0).astype(BF)

    pl.semaphore_wait(barrier, NE - 1 + 4 + 2)
    weights_x(0, w1_in, w1, "start")
    grads = [(cot[...].astype(F32) * wcol[:, k : k + 1]).astype(BF) for k in range(2)]
    gs[...] = (dot(pt[0], grads[0], 0, 0) + dot(pt[1], grads[1], 0, 0)).astype(BF)

    own_rows, mate_rows = pl.ds(0, SLOTS), pl.ds(SLOTS, SLOTS)
    group = 4 * CAP

    def rows_y(k, ref, g):
        src = ref.at[part(g, group)]
        dst = ref.at[part(g + SLOTS // group, group)]
        return remote(src, dst, b_ss.at[k, g], b_rs.at[k, g], row_dev)

    def rows_on(k, ref, dz):
        swap_wait(ref, every, a_rs.at[k], dz)
        rows_y(k, ref, (z + 4 - dz) % 4).start()

    def piece(w, s, h, i):
        return w.at[part((2 * s + h) * 4 + i, HS)]

    def weights_y(m, w, i):
        return remote(piece(w, 0, 0, i), piece(w, 1, 0, i), wy_ss.at[m, i], wy_rs.at[m, i], wgt_dev)

    def weights_core(m, w, s, i):
        return remote(piece(w, s, 0, i), piece(w, s, 1, i), wc_ss.at[m, s, i], wc_rs.at[m, s, i], core_dev)

    def weights_on(m, w, dx):
        i = (x + dx) % 4
        arrived(w.at[part(i, HS)], w_rs.at[m, i])
        weights_y(m, w, i).start()
        weights_core(m, w, 0, i).start()

    def weights_last(m, w):
        for dx in ORDER:
            i = (x + dx) % 4
            weights_y(m, w, i).wait_recv()
            weights_core(m, w, 1, i).start()

    def weights_here(m, w):
        for s in range(2):
            for i in range(4):
                weights_core(m, w, s, i).wait_recv()

    first_w = (lambda: weights_x(0, w1_in, w1, "start"), lambda dx: weights_on(0, w1, dx))
    second_w = (lambda: weights_x(1, w2_in, w2, "start"), lambda dx: weights_on(1, w2, dx))
    first_r = (
        lambda: swap_blocks(xs, x_all, every, a_ss.at[0], a_rs.at[0], "start"),
        lambda dz: rows_on(0, x_all, dz),
    )
    second_r = (
        lambda: swap_blocks(gs, g_all, every, a_ss.at[1], a_rs.at[1], "start"),
        lambda dz: rows_on(1, g_all, dz),
    )
    STAGES = (first_w, first_r, second_r, second_w)
    for begin, _ in STAGES[1:2]:
        begin()
    for stage, (_, land) in enumerate(STAGES):
        for dd in ORDER[:3]:
            land(dd)
        if stage + 2 < len(STAGES):
            STAGES[stage + 2][0]()
        for dd in ORDER[3:]:
            land(dd)
    weights_last(0, w1)
    for g in range(4):
        rows_y(0, x_all, g).wait_recv()
    weights_here(0, w1)

    def tile(j, n=256):
        return pl.ds(pl.multiple_of(j * n, n), n)

    @pl.loop(0, HID // 256)
    def _(j):
        pre = dot(x_all[...], w1[tile(j), :], 1, 1)
        cdf = 0.5 * (1.0 + lax.erf(pre * root_half))
        value = (pre * cdf).astype(BF)
        hid[:, tile(j)] = value
        trans[tile(j), :] = value.T
        slope[:, tile(j)] = cdf + pre * jnp.exp(-0.5 * pre * pre) * density_scale

    for g in range(4):
        rows_y(1, g_all, g).wait_recv()

    def grads_core(m, send, core, s, n):
        return remote(
            send.at[s, :, tile(n)], core.at[s, :, tile(n)], gc_ss.at[m, s, n], gc_rs.at[m, s, n], core_dev
        )

    def grads_y(m, wp, far, n):
        return remote(wp.at[:, tile(n)], far.at[:, tile(n)], gy_ss.at[m, n], gy_rs.at[m, n], wgt_dev)

    def grads_tile(m, right, own, send, core, s, n):
        sums = dot(trans[pl.ds(s * 2 * Q, 2 * Q), :], right[:, tile(n)], 1, 0)
        own[s, :, tile(n)] = sums[:Q]
        send[s, :, tile(n)] = sums[Q:].astype(BF)
        grads_core(m, send, core, s, n).start()

    def weight_grads(m, right, own, send, core, wp, far):
        @pl.loop(0, D // 256)
        def _(n):
            grads_tile(m, right, own, send, core, 1, n)

        @pl.loop(0, D // 256)
        def _(n):
            grads_core(m, send, core, 1, n).wait_recv()
            wp[:, tile(n)] = (own[1, :, tile(n)] + core[1, :, tile(n)].astype(F32)).astype(BF)
            grads_y(m, wp, far, n).start()
            grads_tile(m, right, own, send, core, 0, n)

    def grads_x(m, fin, result, n, act):
        for i in range(4):
            src = fin.at[pl.ds(i * HS, HS), tile(n)]
            dst = result.at[x % 2, part(c, HS), tile(n)]
            rs = gx_rs.at[m, n, 2 * (x % 2) + c]
            own = jnp.logical_and(i == x, c == x // 2)

            @pl.when(own)
            def _():
                if act == "start":
                    pltpu.make_async_copy(src, dst, rs).start()

            @pl.when(jnp.logical_not(own))
            def _():
                copy = remote(src, dst, gx_ss.at[m, n, i], rs, dev(y, i, z, x // 2))
                copy.start() if act == "start" else copy.wait_send()

    def grads_last(m, own, send, core, wp, far, fin, result):
        @pl.loop(0, D // 256)
        def _(n):
            grads_core(m, send, core, 0, n).wait_recv()
            grads_y(m, wp, far, n).wait_recv()
            sums = own[0, :, tile(n)] + core[0, :, tile(n)].astype(F32) + far[:, tile(n)].astype(F32)
            fin[:, tile(n)] = sums.astype(BF)
            grads_x(m, fin, result, n, "start")

    def sums_y(k, send, recv, n):
        return remote(send.at[:, tile(n)], recv.at[:, tile(n)], p_ss.at[k, n], p_rs.at[k, n], row_dev)

    def results_mate(k, left, w, send, recv):
        @pl.loop(0, D // 256)
        def _(n):
            send[:, tile(n)] = dot(left[mate_rows, :], w[:, tile(n)], 1, 0).astype(BF)
            sums_y(k, send, recv, n).start()

    def results_own(k, left, w, send, recv, fin, ret):
        for h, (low, high) in enumerate(SPANS):

            @pl.loop(low, high)
            def _(n):
                own = dot(left[own_rows, :], w[:, tile(n)], 1, 0)
                sums_y(k, send, recv, n).wait_recv()
                fin[:, tile(n)] = (own + recv[:, tile(n)].astype(F32)).astype(BF)

            swap_blocks(fin, ret, span(h), q_ss.at[k, h], q_rs.at[k, h], "start")

    def span(h):
        return pl.ds(SPANS[h][0] * 256, (SPANS[h][1] - SPANS[h][0]) * 256)

    weight_grads(1, g_all, r_own, r_send, r_core, r_wp, r_far)
    weights_last(1, w2)
    weights_here(1, w2)
    results_mate(0, hid, w2, y_send, y_recv)
    @pl.loop(0, HID // 256)
    def _(j):
        back = dot(g_all[...], w2[tile(j), :], 1, 1)
        value = (back * slope[:, tile(j)]).astype(BF)
        dpre[:, tile(j)] = value
        trans[tile(j), :] = value.T

    results_mate(1, dpre, w1, d_send, d_recv)
    weight_grads(0, x_all, e_own, e_send, e_core, e_wp, e_far)
    grads_last(1, r_own, r_send, r_core, r_wp, r_far, r_fin, rg)
    results_own(0, hid, w2, y_send, y_recv, y_fin, y_ret)
    results_own(1, dpre, w1, d_send, d_recv, d_fin, d_ret)
    grads_last(0, e_own, e_send, e_core, e_wp, e_far, e_fin, eg)
    for h in range(len(SPANS)):
        for dz in range(4):
            swap_wait(y_ret, span(h), q_rs.at[0, h], dz)
    result = tok[...].astype(F32)
    for k in range(2):
        pick = dot(pt[k], y_ret[...], 1, 0)
        result = result + pick * wcol[:, k : k + 1]
        inner = acol[...] * jnp.sum(cot[...].astype(F32) * pick, axis=1, keepdims=True)
        gg[k : k + 1, :] = jnp.sum(jnp.where(lane == sub, inner, 0.0), axis=0, keepdims=True)
    out[...] = result.astype(BF)
    for h in range(len(SPANS)):
        for dz in range(4):
            swap_wait(d_ret, span(h), q_rs.at[1, h], dz)
    dnorm = (dot(pt[0], d_ret[...], 1, 0) + dot(pt[1], d_ret[...], 1, 0)) * acol[...]
    tail = dnorm - jnp.mean(dnorm, axis=1, keepdims=True)
    tail = tail - normed[...] * jnp.mean(dnorm * normed[...], axis=1, keepdims=True)
    tg[...] = (cot[...].astype(F32) + inv[...] * tail).astype(BF)


    for m, result in ((1, rg), (0, eg)):

        @pl.loop(0, D // 256)
        def _(n):
            for l in range(2):
                for h in range(2):
                    arrived(result.at[l, pl.ds(h * HS, HS), tile(n)], gx_rs.at[m, n, 2 * l + h])

    for m, (w_in, w) in enumerate(((w1_in, w1), (w2_in, w2))):
        weights_x(m, w_in, w, "wait")
        for i in range(4):
            weights_y(m, w, i).wait_send()
            for s in range(2):
                weights_core(m, w, s, i).wait_send()
    for k, (src, dst) in enumerate(((xs, x_all), (gs, g_all))):
        swap_blocks(src, dst, every, a_ss.at[k], a_rs.at[k], "wait")
        for g in range(4):
            rows_y(k, dst, g).wait_send()
    for k, (send, recv, fin, ret) in enumerate(((y_send, y_recv, y_fin, y_ret), (d_send, d_recv, d_fin, d_ret))):
        for h in range(len(SPANS)):
            swap_blocks(fin, ret, span(h), q_ss.at[k, h], q_rs.at[k, h], "wait")

        @pl.loop(0, D // 256)
        def _(n):
            sums_y(k, send, recv, n).wait_send()

    for m, send, core, wp, far, fin, result in (
        (0, e_send, e_core, e_wp, e_far, e_fin, eg),
        (1, r_send, r_core, r_wp, r_far, r_fin, rg),
    ):

        @pl.loop(0, D // 256)
        def _(n):
            for s in range(2):
                grads_core(m, send, core, s, n).wait_send()
            grads_y(m, wp, far, n).wait_send()
            grads_x(m, fin, result, n, "wait")


def hand_out(*refs):
    sems = refs[-1]
    half = len(refs) // 2
    copies = [pltpu.make_async_copy(refs[i], refs[half + i], sems.at[i]) for i in range(half)]
    for copy in copies:
        copy.start()
    for copy in copies:
        copy.wait()


def body(tokens, cotangent, gate_weights, expert_ids, *rest):
    vmem = pl.BlockSpec(memory_space=pltpu.VMEM)
    hbm = pl.BlockSpec(memory_space=pl.ANY)
    dma = pltpu.SemaphoreType.DMA
    shape = jax.ShapeDtypeStruct
    tiles = D // 256
    grad_scratch = [
        pltpu.VMEM((2, Q, D), F32),
        pltpu.VMEM((2, Q, D), BF),
        pltpu.VMEM((2, Q, D), BF),
        pltpu.VMEM((Q, D), BF),
        pltpu.VMEM((Q, D), BF),
        pltpu.VMEM((Q, D), BF),
    ]
    shapes = (
        shape((TOK, D), BF),
        shape((TOK, D), BF),
        shape((2, TOK), F32),
        shape((2, SH, D), BF),
        shape((2, SH, D), BF),
    )
    results = pl.pallas_call(
        kernel,
        out_shape=shapes,
        in_specs=[vmem] * 6 + [hbm] * 2,
        out_specs=(vmem, vmem, vmem, hbm, hbm),
        scratch_shapes=[
            pltpu.VMEM((2, TOK, SLOTS), BF),
            pltpu.VMEM((TOK, D), F32),
            pltpu.VMEM((TOK, 1), F32),
            pltpu.VMEM((TOK, 2), F32),
            pltpu.VMEM((TOK, 1), F32),
            pltpu.VMEM((SLOTS, D), BF),
            pltpu.VMEM((SLOTS, D), BF),
            pltpu.VMEM((ROWS, D), BF),
            pltpu.VMEM((ROWS, D), BF),
            pltpu.VMEM((HID, D), BF),
            pltpu.VMEM((HID, D), BF),
            pltpu.VMEM((ROWS, HID), BF),
            pltpu.VMEM((ROWS, HID), F32),
            pltpu.VMEM((ROWS, HID), BF),
            pltpu.VMEM((HID, ROWS), BF),
        ]
        + [pltpu.VMEM((SLOTS, D), BF)] * 8
        + grad_scratch * 2
        + [
            dma((2, NE)),
            dma((2, NE)),
            dma((2, 4)),
            dma((2, 4)),
            dma((2, tiles)),
            dma((2, tiles)),
            dma((2, len(SPANS), NE)),
            dma((2, len(SPANS), NE)),
            dma((2, 4)),
            dma((2, 4)),
            dma((2, 4)),
            dma((2, 4)),
            dma((2, 2, 4)),
            dma((2, 2, 4)),
            dma((2, 2, tiles)),
            dma((2, 2, tiles)),
            dma((2, tiles)),
            dma((2, tiles)),
            dma((2, tiles, 4)),
            dma((2, tiles, 4)),
        ],
        compiler_params=pltpu.CompilerParams(
            collective_id=0, has_side_effects=True, vmem_limit_bytes=60 * 2**20
        ),
    )(tokens, cotangent, gate_weights.T, expert_ids.T, *rest)
    out, tg, gg, eg, rg = pl.pallas_call(
        hand_out,
        out_shape=shapes,
        in_specs=[hbm] * 5,
        out_specs=(vmem,) * 5,
        scratch_shapes=[dma((5,))],
    )(*results)
    return out, tg, gg.T, eg, rg


def solution(mesh):
    rows = P(("dp", "expert"), None)
    weights = P("expert", "dp", None)
    return jax.shard_map(
        body,
        mesh=mesh,
        in_specs=(rows,) * 6 + (weights,) * 2,
        out_specs=(rows,) * 3 + (weights,) * 2,
        check_vma=False,
    )
```

```python
import jax
import jax.numpy as jnp
from jax import lax
from jax.experimental import pallas as pl
from jax.experimental.pallas import tpu as pltpu
from jax.sharding import PartitionSpec as P

MESH = pl.DeviceIdType.MESH
epsilon = 1e-06
root_half = 0.7071067811865476
density_scale = 0.3989422804014327

D = 1280
TOK = 128
SLOTS = 256
CAP = 16
NE = 16
SH = 160
HS = SH // 2
Q = 4 * HS
HID = 4 * Q
ROWS = 2 * SLOTS
ORDER = (0, 1, 3, 2)
STAGES = (
    (0, 0, 0),
    (0, 0, 1),
    (0, 1, 0),
    (0, 1, 1),
    (1, 0, 0),
    (1, 0, 1),
    (1, 1, 0),
    (1, 1, 1),
)
HEAD, FLIGHT, LEAD = 2, 3, 3
CUTS = 2
SPANS = ((0, 3), (3, 5))
BF = jnp.bfloat16
F32 = jnp.float32


def dot(a, b, ca, cb):
    return lax.dot_general(a, b, (((ca,), (cb,)), ((), ())), preferred_element_type=F32)


def kernel(
    tok, cot, gw, ids, seg, keep, w1_in, w2_in,
    out, tg, gg, eg, rg,
    pt, normed, inv, wcol, acol, xs, gs, x_all, g_all, w1, w2, hid, slope, dpre, trans,
    y_send, y_recv, y_fin, y_ret, d_send, d_recv, d_fin, d_ret,
    e_own, e_send, e_core, e_wp, e_far, e_fin, r_own, r_send, r_core, r_wp, r_far, r_fin,
    a_ss, a_rs, b_ss, b_rs, p_ss, p_rs, q_ss, q_rs, w_ss, w_rs, wy_ss, wy_rs, wc_ss, wc_rs,
    gc_ss, gc_rs, gy_ss, gy_rs, gx_ss, gx_rs,
):
    dp = lax.axis_index("dp")
    ex = lax.axis_index("expert")
    y, x = dp // 4, dp % 4
    z, c = ex // 2, ex % 2
    row_mate = y + 1 - 2 * (y % 2)
    wgt_mate = (y + 5 - 2 * ((y + 1) % 2)) % 4
    other = 1 - c

    def dev(yy, xx, zz, cc):
        return (yy * 4 + xx, zz * 2 + cc)

    row_dev = dev(row_mate, x, z, c)
    wgt_dev = dev(wgt_mate, x, z, c)
    core_dev = dev(y, x, z, other)

    def remote(src, dst, ss, rs, target):
        return pltpu.make_async_remote_copy(
            src_ref=src, dst_ref=dst, send_sem=ss, recv_sem=rs, device_id=target, device_id_type=MESH
        )

    def arrived(dst, rs):
        pltpu.make_async_copy(dst, dst, rs).wait()

    def part(i, n):
        return pl.ds(pl.multiple_of(i * n, n), n)

    barrier = pltpu.get_barrier_semaphore()
    for dz in range(4):
        for dx in range(4):
            if dz or dx:
                pl.semaphore_signal(
                    barrier, inc=1, device_id=dev(y, (x + dx) % 4, (z + dz) % 4, c), device_id_type=MESH
                )
    for i in range(4):
        pl.semaphore_signal(barrier, inc=1, device_id=dev(y, i, z, other), device_id_type=MESH)
    for target in (row_dev, wgt_dev):
        pl.semaphore_signal(barrier, inc=1, device_id=target, device_id_type=MESH)

    def cut(q):
        return pl.ds(q * (D // CUTS), D // CUTS)

    def weights_x(m, q, w_in, w, act):
        for l in range(2):
            for h in range(2):
                tx = 2 * c + l
                src = w_in.at[l, pl.ds(HS * h, HS), cut(q)]
                dst = w.at[part(x, HS), cut(q)]
                own = jnp.logical_and(tx == x, h == c)

                @pl.when(own)
                def _():
                    if act == "start":
                        pltpu.make_async_copy(src, dst, w_rs.at[m, q, x]).start()

                @pl.when(jnp.logical_not(own))
                def _():
                    copy = remote(
                        src, dst, w_ss.at[m, q, 2 * l + h], w_rs.at[m, q, x], dev(y, tx, z, h)
                    )
                    copy.start() if act == "start" else copy.wait_send()

    def swap_blocks(src, dst, cols, ss, rs, act):
        mine = part(z * 4 + x, CAP)
        for dz in ORDER:
            for dx in ORDER:
                i = dz * 4 + dx
                tx, tz = (x + dx) % 4, (z + dz) % 4
                theirs = part(tz * 4 + tx, CAP)
                if i == 0:
                    if act == "start":
                        pltpu.make_async_copy(src.at[mine, cols], dst.at[mine, cols], rs.at[0]).start()
                else:
                    copy = remote(
                        src.at[theirs, cols], dst.at[mine, cols], ss.at[i], rs.at[i], dev(y, tx, tz, c)
                    )
                    copy.start() if act == "start" else copy.wait_send()

    def swap_wait(dst, cols, rs, dz):
        for dx in range(4):
            block = ((z + 4 - dz) % 4) * 4 + (x + 4 - dx) % 4
            arrived(dst.at[part(block, CAP), cols], rs.at[dz * 4 + dx])

    def begin(m, q, rows):
        if rows:
            swap_blocks((xs, gs)[m], (x_all, g_all)[m], cut(q), a_ss.at[m, q], a_rs.at[m, q], "start")
        else:
            weights_x(m, q, (w1_in, w2_in)[m], (w1, w2)[m], "start")

    lane = lax.broadcasted_iota(jnp.int32, (TOK, TOK), 1)
    sub = lax.broadcasted_iota(jnp.int32, (TOK, TOK), 0)

    def column(row):
        wide_row = jnp.broadcast_to(row.astype(F32), (TOK, TOK))
        return jnp.sum(jnp.where(lane == sub, wide_row, 0.0), axis=1, keepdims=True)

    seg_row = jnp.broadcast_to(seg[...].astype(F32), (TOK, TOK))
    seg_col = column(seg[...])
    earlier = jnp.sum((seg_row < seg_col).astype(F32), axis=1, keepdims=True)
    images = keep.shape[1]
    image = lax.broadcasted_iota(jnp.int32, (TOK, images), 1).astype(F32)
    kept = jnp.broadcast_to(keep[...].astype(F32), (TOK, images))
    keep_token = jnp.sum(jnp.where(image == seg_col, kept, 0.0), axis=1, keepdims=True)
    position = lax.broadcasted_iota(jnp.int32, (TOK, 1), 0).astype(F32)
    alive = (position - earlier < keep_token).astype(F32)
    acol[...] = alive
    expert = lax.broadcasted_iota(jnp.int32, (TOK, NE), 1).astype(F32)
    chosen = [column(ids[k : k + 1, :]) for k in range(2)]
    match = [(chosen[k] == expert).astype(F32) for k in range(2)]
    before = dot((lane < sub).astype(BF), (match[0] + match[1]).astype(BF), 1, 0)
    slot_iota = lax.broadcasted_iota(jnp.int32, (TOK, SLOTS), 1).astype(F32)
    for k in range(2):
        wcol[:, k : k + 1] = column(gw[k : k + 1, :]) * alive
        slot = jnp.sum(before * match[k], axis=1, keepdims=True)
        if k == 1:
            slot = slot + jnp.sum(match[0] * match[1], axis=1, keepdims=True)
        pt[k] = (slot_iota == chosen[k] * CAP + slot).astype(BF)

    wide = tok[...].astype(F32)
    centred = wide - jnp.mean(wide, axis=1, keepdims=True)
    scale = lax.rsqrt(jnp.mean(centred * centred, axis=1, keepdims=True) + epsilon)
    inv[...] = scale
    normed[...] = centred * scale
    feats = (normed[...].astype(BF).astype(F32) * alive).astype(BF)
    xs[...] = dot(pt[0] + pt[1], feats, 0, 0).astype(BF)

    pl.semaphore_wait(barrier, NE - 1 + 4 + 2)
    for stage in STAGES[:HEAD]:
        begin(*stage)
    grads = [(cot[...].astype(F32) * wcol[:, k : k + 1]).astype(BF) for k in range(2)]
    gs[...] = (dot(pt[0], grads[0], 0, 0) + dot(pt[1], grads[1], 0, 0)).astype(BF)

    own_rows, mate_rows = pl.ds(0, SLOTS), pl.ds(SLOTS, SLOTS)
    group = 4 * CAP

    def rows_y(k, q, ref, g):
        src = ref.at[part(g, group), cut(q)]
        dst = ref.at[part(g + SLOTS // group, group), cut(q)]
        return remote(src, dst, b_ss.at[k, q, g], b_rs.at[k, q, g], row_dev)

    def rows_on(k, q, ref, dz):
        swap_wait(ref, cut(q), a_rs.at[k, q], dz)
        rows_y(k, q, ref, (z + 4 - dz) % 4).start()

    def piece(w, q, s, h, i):
        return w.at[part((2 * s + h) * 4 + i, HS), cut(q)]

    def weights_y(m, q, w, i):
        return remote(
            piece(w, q, 0, 0, i), piece(w, q, 1, 0, i), wy_ss.at[m, q, i], wy_rs.at[m, q, i], wgt_dev
        )

    def weights_core(m, q, w, s, i):
        return remote(
            piece(w, q, s, 0, i), piece(w, q, s, 1, i), wc_ss.at[m, q, s, i], wc_rs.at[m, q, s, i], core_dev
        )

    def weights_on(m, q, w, dx):
        i = (x + dx) % 4
        arrived(w.at[part(i, HS), cut(q)], w_rs.at[m, q, i])
        weights_y(m, q, w, i).start()
        weights_core(m, q, w, 0, i).start()

    def weights_last(m, w):
        for q in range(CUTS):
            for dx in ORDER:
                i = (x + dx) % 4
                weights_y(m, q, w, i).wait_recv()
                weights_core(m, q, w, 1, i).start()

    def weights_here(m, w):
        for q in range(CUTS):
            for s in range(2):
                for i in range(4):
                    weights_core(m, q, w, s, i).wait_recv()

    def land(m, q, rows, dd):
        if rows:
            rows_on(m, q, (x_all, g_all)[m], dd)
        else:
            weights_on(m, q, (w1, w2)[m], dd)

    for stage in STAGES[HEAD:FLIGHT]:
        begin(*stage)
    for n, stage in enumerate(STAGES):
        for dd in ORDER[:LEAD]:
            land(*stage, dd)
        if n + FLIGHT < len(STAGES):
            begin(*STAGES[n + FLIGHT])
        for dd in ORDER[LEAD:]:
            land(*stage, dd)
    weights_last(0, w1)
    for q in range(CUTS):
        for g in range(4):
            rows_y(0, q, x_all, g).wait_recv()
    weights_here(0, w1)

    def tile(j, n=256):
        return pl.ds(pl.multiple_of(j * n, n), n)

    @pl.loop(0, HID // 256)
    def _(j):
        pre = dot(x_all[...], w1[tile(j), :], 1, 1)
        cdf = 0.5 * (1.0 + lax.erf(pre * root_half))
        value = (pre * cdf).astype(BF)
        hid[:, tile(j)] = value
        trans[tile(j), :] = value.T
        slope[:, tile(j)] = cdf + pre * jnp.exp(-0.5 * pre * pre) * density_scale


    def grads_core(m, send, core, s, n):
        return remote(
            send.at[s, :, tile(n)], core.at[s, :, tile(n)], gc_ss.at[m, s, n], gc_rs.at[m, s, n], core_dev
        )

    def grads_y(m, wp, far, n):
        return remote(wp.at[:, tile(n)], far.at[:, tile(n)], gy_ss.at[m, n], gy_rs.at[m, n], wgt_dev)

    def grads_tile(m, right, own, send, core, s, n):
        sums = dot(trans[pl.ds(s * 2 * Q, 2 * Q), :], right[:, tile(n)], 1, 0)
        own[s, :, tile(n)] = sums[:Q]
        send[s, :, tile(n)] = sums[Q:].astype(BF)
        grads_core(m, send, core, s, n).start()

    def weight_grads(m, right, own, send, core, wp, far):
        @pl.loop(0, D // 256)
        def _(n):
            grads_tile(m, right, own, send, core, 1, n)

        @pl.loop(0, D // 256)
        def _(n):
            grads_core(m, send, core, 1, n).wait_recv()
            wp[:, tile(n)] = (own[1, :, tile(n)] + core[1, :, tile(n)].astype(F32)).astype(BF)
            grads_y(m, wp, far, n).start()
            grads_tile(m, right, own, send, core, 0, n)

    def grads_x(m, fin, result, n, act):
        for i in range(4):
            src = fin.at[pl.ds(i * HS, HS), tile(n)]
            dst = result.at[x % 2, part(c, HS), tile(n)]
            rs = gx_rs.at[m, n, 2 * (x % 2) + c]
            own = jnp.logical_and(i == x, c == x // 2)

            @pl.when(own)
            def _():
                if act == "start":
                    pltpu.make_async_copy(src, dst, rs).start()

            @pl.when(jnp.logical_not(own))
            def _():
                copy = remote(src, dst, gx_ss.at[m, n, i], rs, dev(y, i, z, x // 2))
                copy.start() if act == "start" else copy.wait_send()

    def grads_last(m, own, send, core, wp, far, fin, result):
        @pl.loop(0, D // 256)
        def _(n):
            grads_core(m, send, core, 0, n).wait_recv()
            grads_y(m, wp, far, n).wait_recv()
            sums = own[0, :, tile(n)] + core[0, :, tile(n)].astype(F32) + far[:, tile(n)].astype(F32)
            fin[:, tile(n)] = sums.astype(BF)
            grads_x(m, fin, result, n, "start")

    def sums_y(k, send, recv, n):
        return remote(send.at[:, tile(n)], recv.at[:, tile(n)], p_ss.at[k, n], p_rs.at[k, n], row_dev)

    def results_mate(k, left, w, send, recv):
        @pl.loop(0, D // 256)
        def _(n):
            send[:, tile(n)] = dot(left[mate_rows, :], w[:, tile(n)], 1, 0).astype(BF)
            sums_y(k, send, recv, n).start()

    def results_own(k, left, w, send, recv, fin, ret):
        for h, (low, high) in enumerate(SPANS):

            @pl.loop(low, high)
            def _(n):
                own = dot(left[own_rows, :], w[:, tile(n)], 1, 0)
                sums_y(k, send, recv, n).wait_recv()
                fin[:, tile(n)] = (own + recv[:, tile(n)].astype(F32)).astype(BF)

            swap_blocks(fin, ret, span(h), q_ss.at[k, h], q_rs.at[k, h], "start")

    def span(h):
        return pl.ds(SPANS[h][0] * 256, (SPANS[h][1] - SPANS[h][0]) * 256)

    for q in range(CUTS):
        for g in range(4):
            rows_y(1, q, g_all, g).wait_recv()
    weights_last(1, w2)
    weight_grads(1, g_all, r_own, r_send, r_core, r_wp, r_far)
    weights_here(1, w2)
    results_mate(0, hid, w2, y_send, y_recv)
    @pl.loop(0, HID // 256)
    def _(j):
        back = dot(g_all[...], w2[tile(j), :], 1, 1)
        value = (back * slope[:, tile(j)]).astype(BF)
        dpre[:, tile(j)] = value
        trans[tile(j), :] = value.T

    results_mate(1, dpre, w1, d_send, d_recv)
    weight_grads(0, x_all, e_own, e_send, e_core, e_wp, e_far)
    grads_last(1, r_own, r_send, r_core, r_wp, r_far, r_fin, rg)
    results_own(0, hid, w2, y_send, y_recv, y_fin, y_ret)
    results_own(1, dpre, w1, d_send, d_recv, d_fin, d_ret)
    grads_last(0, e_own, e_send, e_core, e_wp, e_far, e_fin, eg)
    for h in range(len(SPANS)):
        for dz in range(4):
            swap_wait(y_ret, span(h), q_rs.at[0, h], dz)
    result = tok[...].astype(F32)
    for k in range(2):
        pick = dot(pt[k], y_ret[...], 1, 0)
        result = result + pick * wcol[:, k : k + 1]
        inner = acol[...] * jnp.sum(cot[...].astype(F32) * pick, axis=1, keepdims=True)
        gg[k : k + 1, :] = jnp.sum(jnp.where(lane == sub, inner, 0.0), axis=0, keepdims=True)
    out[...] = result.astype(BF)
    for h in range(len(SPANS)):
        for dz in range(4):
            swap_wait(d_ret, span(h), q_rs.at[1, h], dz)
    dnorm = (dot(pt[0], d_ret[...], 1, 0) + dot(pt[1], d_ret[...], 1, 0)) * acol[...]
    tail = dnorm - jnp.mean(dnorm, axis=1, keepdims=True)
    tail = tail - normed[...] * jnp.mean(dnorm * normed[...], axis=1, keepdims=True)
    tg[...] = (cot[...].astype(F32) + inv[...] * tail).astype(BF)


    for m, result in ((1, rg), (0, eg)):

        @pl.loop(0, D // 256)
        def _(n):
            for l in range(2):
                for h in range(2):
                    arrived(result.at[l, pl.ds(h * HS, HS), tile(n)], gx_rs.at[m, n, 2 * l + h])

    for m, (w_in, w) in enumerate(((w1_in, w1), (w2_in, w2))):
        for q in range(CUTS):
            weights_x(m, q, w_in, w, "wait")
            for i in range(4):
                weights_y(m, q, w, i).wait_send()
                for s in range(2):
                    weights_core(m, q, w, s, i).wait_send()
    for k, (src, dst) in enumerate(((xs, x_all), (gs, g_all))):
        for q in range(CUTS):
            swap_blocks(src, dst, cut(q), a_ss.at[k, q], a_rs.at[k, q], "wait")
            for g in range(4):
                rows_y(k, q, dst, g).wait_send()
    for k, (send, recv, fin, ret) in enumerate(((y_send, y_recv, y_fin, y_ret), (d_send, d_recv, d_fin, d_ret))):
        for h in range(len(SPANS)):
            swap_blocks(fin, ret, span(h), q_ss.at[k, h], q_rs.at[k, h], "wait")

        @pl.loop(0, D // 256)
        def _(n):
            sums_y(k, send, recv, n).wait_send()

    for m, send, core, wp, far, fin, result in (
        (0, e_send, e_core, e_wp, e_far, e_fin, eg),
        (1, r_send, r_core, r_wp, r_far, r_fin, rg),
    ):

        @pl.loop(0, D // 256)
        def _(n):
            for s in range(2):
                grads_core(m, send, core, s, n).wait_send()
            grads_y(m, wp, far, n).wait_send()
            grads_x(m, fin, result, n, "wait")


def hand_out(*refs):
    sems = refs[-1]
    half = len(refs) // 2
    copies = [pltpu.make_async_copy(refs[i], refs[half + i], sems.at[i]) for i in range(half)]
    for copy in copies:
        copy.start()
    for copy in copies:
        copy.wait()


def body(tokens, cotangent, gate_weights, expert_ids, *rest):
    vmem = pl.BlockSpec(memory_space=pltpu.VMEM)
    hbm = pl.BlockSpec(memory_space=pl.ANY)
    dma = pltpu.SemaphoreType.DMA
    shape = jax.ShapeDtypeStruct
    tiles = D // 256
    grad_scratch = [
        pltpu.VMEM((2, Q, D), F32),
        pltpu.VMEM((2, Q, D), BF),
        pltpu.VMEM((2, Q, D), BF),
        pltpu.VMEM((Q, D), BF),
        pltpu.VMEM((Q, D), BF),
        pltpu.VMEM((Q, D), BF),
    ]
    shapes = (
        shape((TOK, D), BF),
        shape((TOK, D), BF),
        shape((2, TOK), F32),
        shape((2, SH, D), BF),
        shape((2, SH, D), BF),
    )
    results = pl.pallas_call(
        kernel,
        out_shape=shapes,
        in_specs=[vmem] * 6 + [hbm] * 2,
        out_specs=(vmem, vmem, vmem, hbm, hbm),
        scratch_shapes=[
            pltpu.VMEM((2, TOK, SLOTS), BF),
            pltpu.VMEM((TOK, D), F32),
            pltpu.VMEM((TOK, 1), F32),
            pltpu.VMEM((TOK, 2), F32),
            pltpu.VMEM((TOK, 1), F32),
            pltpu.VMEM((SLOTS, D), BF),
            pltpu.VMEM((SLOTS, D), BF),
            pltpu.VMEM((ROWS, D), BF),
            pltpu.VMEM((ROWS, D), BF),
            pltpu.VMEM((HID, D), BF),
            pltpu.VMEM((HID, D), BF),
            pltpu.VMEM((ROWS, HID), BF),
            pltpu.VMEM((ROWS, HID), F32),
            pltpu.VMEM((ROWS, HID), BF),
            pltpu.VMEM((HID, ROWS), BF),
        ]
        + [pltpu.VMEM((SLOTS, D), BF)] * 8
        + grad_scratch * 2
        + [
            dma((2, CUTS, NE)),
            dma((2, CUTS, NE)),
            dma((2, CUTS, 4)),
            dma((2, CUTS, 4)),
            dma((2, tiles)),
            dma((2, tiles)),
            dma((2, len(SPANS), NE)),
            dma((2, len(SPANS), NE)),
            dma((2, CUTS, 4)),
            dma((2, CUTS, 4)),
            dma((2, CUTS, 4)),
            dma((2, CUTS, 4)),
            dma((2, CUTS, 2, 4)),
            dma((2, CUTS, 2, 4)),
            dma((2, 2, tiles)),
            dma((2, 2, tiles)),
            dma((2, tiles)),
            dma((2, tiles)),
            dma((2, tiles, 4)),
            dma((2, tiles, 4)),
        ],
        compiler_params=pltpu.CompilerParams(
            collective_id=0, has_side_effects=True, vmem_limit_bytes=60 * 2**20
        ),
    )(tokens, cotangent, gate_weights.T, expert_ids.T, *rest)
    out, tg, gg, eg, rg = pl.pallas_call(
        hand_out,
        out_shape=shapes,
        in_specs=[hbm] * 5,
        out_specs=(vmem,) * 5,
        scratch_shapes=[dma((5,))],
    )(*results)
    return out, tg, gg.T, eg, rg


def solution(mesh):
    rows = P(("dp", "expert"), None)
    weights = P("expert", "dp", None)
    return jax.shard_map(
        body,
        mesh=mesh,
        in_specs=(rows,) * 6 + (weights,) * 2,
        out_specs=(rows,) * 3 + (weights,) * 2,
        check_vma=False,
    )
```

```python
import jax
import jax.numpy as jnp
from jax import lax
from jax.experimental import pallas as pl
from jax.experimental.pallas import tpu as pltpu
from jax.sharding import PartitionSpec as P

MESH = pl.DeviceIdType.MESH
epsilon = 1e-06
root_half = 0.7071067811865476
density_scale = 0.3989422804014327

D = 1280
TOK = 128
SLOTS = 256
CAP = 16
NE = 16
SH = 160
HS = SH // 2
Q = 4 * HS
HID = 4 * Q
ROWS = 2 * SLOTS
ORDER = (0, 1, 3, 2)
STAGES = (
    (0, 0, 0),
    (0, 0, 1),
    (0, 1, 0),
    (0, 1, 1),
    (1, 0, 0),
    (1, 0, 1),
    (1, 1, 0),
    (1, 1, 1),
)
HEAD, FLIGHT, LEAD = 2, 3, 3
CUTS = 2
SPANS = ((0, 3), (3, 5))
BF = jnp.bfloat16
F32 = jnp.float32


def dot(a, b, ca, cb):
    return lax.dot_general(a, b, (((ca,), (cb,)), ((), ())), preferred_element_type=F32)


def kernel(
    tok, cot, gw, ids, seg, keep, w1_in, w2_in,
    out, tg, gg, eg, rg,
    pt, normed, inv, wcol, acol, xs, gs, x_all, g_all, w1, w2, hid, slope, dpre, trans,
    y_send, y_recv, y_fin, y_ret, d_send, d_recv, d_fin, d_ret,
    e_own, e_send, e_core, e_wp, e_far, e_fin, r_own, r_send, r_core, r_wp, r_far, r_fin,
    a_ss, a_rs, b_ss, b_rs, p_ss, p_rs, q_ss, q_rs, w_ss, w_rs, wy_ss, wy_rs, wc_ss, wc_rs,
    gc_ss, gc_rs, gy_ss, gy_rs, gx_ss, gx_rs,
):
    dp = lax.axis_index("dp")
    ex = lax.axis_index("expert")
    y, x = dp // 4, dp % 4
    z, c = ex // 2, ex % 2
    row_mate = y + 1 - 2 * (y % 2)
    wgt_mate = (y + 5 - 2 * ((y + 1) % 2)) % 4
    other = 1 - c

    def dev(yy, xx, zz, cc):
        return (yy * 4 + xx, zz * 2 + cc)

    row_dev = dev(row_mate, x, z, c)
    wgt_dev = dev(wgt_mate, x, z, c)
    core_dev = dev(y, x, z, other)

    def remote(src, dst, ss, rs, target):
        return pltpu.make_async_remote_copy(
            src_ref=src, dst_ref=dst, send_sem=ss, recv_sem=rs, device_id=target, device_id_type=MESH
        )

    def arrived(dst, rs):
        pltpu.make_async_copy(dst, dst, rs).wait()

    def part(i, n):
        return pl.ds(pl.multiple_of(i * n, n), n)

    barrier = pltpu.get_barrier_semaphore()
    for dz in range(4):
        for dx in range(4):
            if dz or dx:
                pl.semaphore_signal(
                    barrier, inc=1, device_id=dev(y, (x + dx) % 4, (z + dz) % 4, c), device_id_type=MESH
                )
    for i in range(4):
        pl.semaphore_signal(barrier, inc=1, device_id=dev(y, i, z, other), device_id_type=MESH)
    for target in (row_dev, wgt_dev):
        pl.semaphore_signal(barrier, inc=1, device_id=target, device_id_type=MESH)

    def cut(q):
        return pl.ds(q * (D // CUTS), D // CUTS)

    def weights_x(m, q, w_in, w, act):
        for l in range(2):
            for h in range(2):
                tx = 2 * c + l
                src = w_in.at[l, pl.ds(HS * h, HS), cut(q)]
                dst = w.at[part(x, HS), cut(q)]
                own = jnp.logical_and(tx == x, h == c)

                @pl.when(own)
                def _():
                    if act == "start":
                        pltpu.make_async_copy(src, dst, w_rs.at[m, q, x]).start()

                @pl.when(jnp.logical_not(own))
                def _():
                    copy = remote(
                        src, dst, w_ss.at[m, q, 2 * l + h], w_rs.at[m, q, x], dev(y, tx, z, h)
                    )
                    copy.start() if act == "start" else copy.wait_send()

    def swap_blocks(src, dst, cols, ss, rs, act):
        mine = part(z * 4 + x, CAP)
        for dz in ORDER:
            for dx in ORDER:
                i = dz * 4 + dx
                tx, tz = (x + dx) % 4, (z + dz) % 4
                theirs = part(tz * 4 + tx, CAP)
                if i == 0:
                    if act == "start":
                        pltpu.make_async_copy(src.at[mine, cols], dst.at[mine, cols], rs.at[0]).start()
                else:
                    copy = remote(
                        src.at[theirs, cols], dst.at[mine, cols], ss.at[i], rs.at[i], dev(y, tx, tz, c)
                    )
                    copy.start() if act == "start" else copy.wait_send()

    def swap_wait(dst, cols, rs, dz):
        for dx in range(4):
            block = ((z + 4 - dz) % 4) * 4 + (x + 4 - dx) % 4
            arrived(dst.at[part(block, CAP), cols], rs.at[dz * 4 + dx])

    def begin(m, q, rows):
        if rows:
            swap_blocks((xs, gs)[m], (x_all, g_all)[m], cut(q), a_ss.at[m, q], a_rs.at[m, q], "start")
        else:
            weights_x(m, q, (w1_in, w2_in)[m], (w1, w2)[m], "start")

    lane = lax.broadcasted_iota(jnp.int32, (TOK, TOK), 1)
    sub = lax.broadcasted_iota(jnp.int32, (TOK, TOK), 0)

    def column(row):
        wide_row = jnp.broadcast_to(row.astype(F32), (TOK, TOK))
        return jnp.sum(jnp.where(lane == sub, wide_row, 0.0), axis=1, keepdims=True)

    seg_row = jnp.broadcast_to(seg[...].astype(F32), (TOK, TOK))
    seg_col = column(seg[...])
    earlier = jnp.sum((seg_row < seg_col).astype(F32), axis=1, keepdims=True)
    images = keep.shape[1]
    image = lax.broadcasted_iota(jnp.int32, (TOK, images), 1).astype(F32)
    kept = jnp.broadcast_to(keep[...].astype(F32), (TOK, images))
    keep_token = jnp.sum(jnp.where(image == seg_col, kept, 0.0), axis=1, keepdims=True)
    position = lax.broadcasted_iota(jnp.int32, (TOK, 1), 0).astype(F32)
    alive = (position - earlier < keep_token).astype(F32)
    acol[...] = alive
    expert = lax.broadcasted_iota(jnp.int32, (TOK, NE), 1).astype(F32)
    chosen = [column(ids[k : k + 1, :]) for k in range(2)]
    match = [(chosen[k] == expert).astype(F32) for k in range(2)]
    before = dot((lane < sub).astype(BF), (match[0] + match[1]).astype(BF), 1, 0)
    slot_iota = lax.broadcasted_iota(jnp.int32, (TOK, SLOTS), 1).astype(F32)
    for k in range(2):
        wcol[:, k : k + 1] = column(gw[k : k + 1, :]) * alive
        slot = jnp.sum(before * match[k], axis=1, keepdims=True)
        if k == 1:
            slot = slot + jnp.sum(match[0] * match[1], axis=1, keepdims=True)
        pt[k] = (slot_iota == chosen[k] * CAP + slot).astype(BF)

    wide = tok[...].astype(F32)
    centred = wide - jnp.mean(wide, axis=1, keepdims=True)
    scale = lax.rsqrt(jnp.mean(centred * centred, axis=1, keepdims=True) + epsilon)
    inv[...] = scale
    normed[...] = centred * scale
    feats = (normed[...].astype(BF).astype(F32) * alive).astype(BF)
    xs[...] = dot(pt[0] + pt[1], feats, 0, 0).astype(BF)

    pl.semaphore_wait(barrier, NE - 1 + 4 + 2)
    for stage in STAGES[:HEAD]:
        begin(*stage)
    grads = [(cot[...].astype(F32) * wcol[:, k : k + 1]).astype(BF) for k in range(2)]
    gs[...] = (dot(pt[0], grads[0], 0, 0) + dot(pt[1], grads[1], 0, 0)).astype(BF)

    own_rows, mate_rows = pl.ds(0, SLOTS), pl.ds(SLOTS, SLOTS)
    group = 4 * CAP

    def rows_y(k, q, ref, g):
        src = ref.at[part(g, group), cut(q)]
        dst = ref.at[part(g + SLOTS // group, group), cut(q)]
        return remote(src, dst, b_ss.at[k, q, g], b_rs.at[k, q, g], row_dev)

    def rows_on(k, q, ref, dz):
        swap_wait(ref, cut(q), a_rs.at[k, q], dz)
        rows_y(k, q, ref, (z + 4 - dz) % 4).start()

    def piece(w, q, s, h, i):
        return w.at[part((2 * s + h) * 4 + i, HS), cut(q)]

    def weights_y(m, q, w, i):
        return remote(
            piece(w, q, 0, 0, i), piece(w, q, 1, 0, i), wy_ss.at[m, q, i], wy_rs.at[m, q, i], wgt_dev
        )

    def weights_core(m, q, w, s, i):
        return remote(
            piece(w, q, s, 0, i), piece(w, q, s, 1, i), wc_ss.at[m, q, s, i], wc_rs.at[m, q, s, i], core_dev
        )

    def weights_on(m, q, w, dx):
        i = (x + dx) % 4
        arrived(w.at[part(i, HS), cut(q)], w_rs.at[m, q, i])
        weights_y(m, q, w, i).start()
        weights_core(m, q, w, 0, i).start()

    def weights_last(m, w):
        for q in range(CUTS):
            for dx in ORDER:
                i = (x + dx) % 4
                weights_y(m, q, w, i).wait_recv()
                weights_core(m, q, w, 1, i).start()

    def weights_here(m, w):
        for q in range(CUTS):
            for s in range(2):
                for i in range(4):
                    weights_core(m, q, w, s, i).wait_recv()

    def land(m, q, rows, dd):
        if rows:
            rows_on(m, q, (x_all, g_all)[m], dd)
        else:
            weights_on(m, q, (w1, w2)[m], dd)

    for stage in STAGES[HEAD:FLIGHT]:
        begin(*stage)
    for n, stage in enumerate(STAGES):
        for dd in ORDER[:LEAD]:
            land(*stage, dd)
        if n + FLIGHT < len(STAGES):
            begin(*STAGES[n + FLIGHT])
        for dd in ORDER[LEAD:]:
            land(*stage, dd)
    weights_last(0, w1)
    for q in range(CUTS):
        for g in range(4):
            rows_y(0, q, x_all, g).wait_recv()
    weights_here(0, w1)

    def tile(j, n=256):
        return pl.ds(pl.multiple_of(j * n, n), n)

    @pl.loop(0, HID // 256)
    def _(j):
        pre = dot(x_all[...], w1[tile(j), :], 1, 1)
        cdf = 0.5 * (1.0 + lax.erf(pre * root_half))
        value = (pre * cdf).astype(BF)
        hid[:, tile(j)] = value
        trans[tile(j), :] = value.T
        slope[:, tile(j)] = cdf + pre * jnp.exp(-0.5 * pre * pre) * density_scale


    def grads_core(m, send, core, s, n):
        return remote(
            send.at[s, :, tile(n)], core.at[s, :, tile(n)], gc_ss.at[m, s, n], gc_rs.at[m, s, n], core_dev
        )

    def grads_y(m, wp, far, n):
        return remote(wp.at[:, tile(n)], far.at[:, tile(n)], gy_ss.at[m, n], gy_rs.at[m, n], wgt_dev)

    def grads_tile(m, right, own, send, core, s, n):
        sums = dot(trans[pl.ds(s * 2 * Q, 2 * Q), :], right[:, tile(n)], 1, 0)
        own[s, :, tile(n)] = sums[:Q]
        send[s, :, tile(n)] = sums[Q:].astype(BF)
        grads_core(m, send, core, s, n).start()

    def weight_grads(m, right, own, send, core, wp, far):
        @pl.loop(0, D // 256)
        def _(n):
            grads_tile(m, right, own, send, core, 1, n)

        @pl.loop(0, D // 256)
        def _(n):
            grads_core(m, send, core, 1, n).wait_recv()
            wp[:, tile(n)] = (own[1, :, tile(n)] + core[1, :, tile(n)].astype(F32)).astype(BF)
            grads_y(m, wp, far, n).start()
            grads_tile(m, right, own, send, core, 0, n)

    def grads_x(m, fin, result, n, act):
        for i in range(4):
            src = fin.at[pl.ds(i * HS, HS), tile(n)]
            dst = result.at[x % 2, part(c, HS), tile(n)]
            rs = gx_rs.at[m, n, 2 * (x % 2) + c]
            own = jnp.logical_and(i == x, c == x // 2)

            @pl.when(own)
            def _():
                if act == "start":
                    pltpu.make_async_copy(src, dst, rs).start()

            @pl.when(jnp.logical_not(own))
            def _():
                copy = remote(src, dst, gx_ss.at[m, n, i], rs, dev(y, i, z, x // 2))
                copy.start() if act == "start" else copy.wait_send()

    def grads_last(m, own, send, core, wp, far, fin, result):
        @pl.loop(0, D // 256)
        def _(n):
            grads_core(m, send, core, 0, n).wait_recv()
            grads_y(m, wp, far, n).wait_recv()
            sums = own[0, :, tile(n)] + core[0, :, tile(n)].astype(F32) + far[:, tile(n)].astype(F32)
            fin[:, tile(n)] = sums.astype(BF)
            grads_x(m, fin, result, n, "start")

    def sums_y(k, send, recv, n):
        return remote(send.at[:, tile(n)], recv.at[:, tile(n)], p_ss.at[k, n], p_rs.at[k, n], row_dev)

    def results_mate(k, left, w, send, recv):
        @pl.loop(0, D // 256)
        def _(n):
            send[:, tile(n)] = dot(left[mate_rows, :], w[:, tile(n)], 1, 0).astype(BF)
            sums_y(k, send, recv, n).start()

    def results_own(k, left, w, send, recv, fin, ret):
        for h, (low, high) in enumerate(SPANS):

            @pl.loop(low, high)
            def _(n):
                own = dot(left[own_rows, :], w[:, tile(n)], 1, 0)
                sums_y(k, send, recv, n).wait_recv()
                fin[:, tile(n)] = (own + recv[:, tile(n)].astype(F32)).astype(BF)

            swap_blocks(fin, ret, span(h), q_ss.at[k, h], q_rs.at[k, h], "start")

    def span(h):
        return pl.ds(SPANS[h][0] * 256, (SPANS[h][1] - SPANS[h][0]) * 256)

    for q in range(CUTS):
        for g in range(4):
            rows_y(1, q, g_all, g).wait_recv()
    weights_last(1, w2)
    weight_grads(1, g_all, r_own, r_send, r_core, r_wp, r_far)
    weights_here(1, w2)
    results_mate(0, hid, w2, y_send, y_recv)
    @pl.loop(0, HID // 256)
    def _(j):
        back = dot(g_all[...], w2[tile(j), :], 1, 1)
        value = (back * slope[:, tile(j)]).astype(BF)
        dpre[:, tile(j)] = value
        trans[tile(j), :] = value.T

    results_mate(1, dpre, w1, d_send, d_recv)
    weight_grads(0, x_all, e_own, e_send, e_core, e_wp, e_far)
    grads_last(1, r_own, r_send, r_core, r_wp, r_far, r_fin, rg)
    results_own(0, hid, w2, y_send, y_recv, y_fin, y_ret)
    results_own(1, dpre, w1, d_send, d_recv, d_fin, d_ret)
    grads_last(0, e_own, e_send, e_core, e_wp, e_far, e_fin, eg)
    for h in range(len(SPANS)):
        for dz in range(4):
            swap_wait(y_ret, span(h), q_rs.at[0, h], dz)
    result = tok[...].astype(F32)
    for k in range(2):
        pick = dot(pt[k], y_ret[...], 1, 0)
        result = result + pick * wcol[:, k : k + 1]
        inner = acol[...] * jnp.sum(cot[...].astype(F32) * pick, axis=1, keepdims=True)
        gg[k : k + 1, :] = jnp.sum(jnp.where(lane == sub, inner, 0.0), axis=0, keepdims=True)
    out[...] = result.astype(BF)
    for h in range(len(SPANS)):
        for dz in range(4):
            swap_wait(d_ret, span(h), q_rs.at[1, h], dz)
    dnorm = (dot(pt[0], d_ret[...], 1, 0) + dot(pt[1], d_ret[...], 1, 0)) * acol[...]
    tail = dnorm - jnp.mean(dnorm, axis=1, keepdims=True)
    tail = tail - normed[...] * jnp.mean(dnorm * normed[...], axis=1, keepdims=True)
    tg[...] = (cot[...].astype(F32) + inv[...] * tail).astype(BF)


    for m, result in ((1, rg), (0, eg)):

        @pl.loop(0, D // 256)
        def _(n):
            for l in range(2):
                for h in range(2):
                    arrived(result.at[l, pl.ds(h * HS, HS), tile(n)], gx_rs.at[m, n, 2 * l + h])

    for m, (w_in, w) in enumerate(((w1_in, w1), (w2_in, w2))):
        for q in range(CUTS):
            weights_x(m, q, w_in, w, "wait")
            for i in range(4):
                weights_y(m, q, w, i).wait_send()
                for s in range(2):
                    weights_core(m, q, w, s, i).wait_send()
    for k, (src, dst) in enumerate(((xs, x_all), (gs, g_all))):
        for q in range(CUTS):
            swap_blocks(src, dst, cut(q), a_ss.at[k, q], a_rs.at[k, q], "wait")
            for g in range(4):
                rows_y(k, q, dst, g).wait_send()
    for k, (send, recv, fin, ret) in enumerate(((y_send, y_recv, y_fin, y_ret), (d_send, d_recv, d_fin, d_ret))):
        for h in range(len(SPANS)):
            swap_blocks(fin, ret, span(h), q_ss.at[k, h], q_rs.at[k, h], "wait")

        @pl.loop(0, D // 256)
        def _(n):
            sums_y(k, send, recv, n).wait_send()

    for m, send, core, wp, far, fin, result in (
        (0, e_send, e_core, e_wp, e_far, e_fin, eg),
        (1, r_send, r_core, r_wp, r_far, r_fin, rg),
    ):

        @pl.loop(0, D // 256)
        def _(n):
            for s in range(2):
                grads_core(m, send, core, s, n).wait_send()
            grads_y(m, wp, far, n).wait_send()
            grads_x(m, fin, result, n, "wait")


def hand_out(*refs):
    sems = refs[-1]
    ins, outs, held = refs[:5], refs[5:10], refs[10:15]
    order = (2, 0, 1, 3, 4)
    inward = [pltpu.make_async_copy(ins[i], held[i], sems.at[0, i]) for i in order]
    outward = [pltpu.make_async_copy(held[i], outs[i], sems.at[1, i]) for i in order]
    for copy in inward:
        copy.start()
    for first, second in zip(inward, outward):
        first.wait()
        second.start()
    for copy in outward:
        copy.wait()


def body(tokens, cotangent, gate_weights, expert_ids, *rest):
    vmem = pl.BlockSpec(memory_space=pltpu.VMEM)
    hbm = pl.BlockSpec(memory_space=pl.ANY)
    dma = pltpu.SemaphoreType.DMA
    shape = jax.ShapeDtypeStruct
    tiles = D // 256
    grad_scratch = [
        pltpu.VMEM((2, Q, D), F32),
        pltpu.VMEM((2, Q, D), BF),
        pltpu.VMEM((2, Q, D), BF),
        pltpu.VMEM((Q, D), BF),
        pltpu.VMEM((Q, D), BF),
        pltpu.VMEM((Q, D), BF),
    ]
    shapes = (
        shape((TOK, D), BF),
        shape((TOK, D), BF),
        shape((2, TOK), F32),
        shape((2, SH, D), BF),
        shape((2, SH, D), BF),
    )
    results = pl.pallas_call(
        kernel,
        out_shape=shapes,
        in_specs=[vmem] * 6 + [hbm] * 2,
        out_specs=(vmem, vmem, vmem, hbm, hbm),
        scratch_shapes=[
            pltpu.VMEM((2, TOK, SLOTS), BF),
            pltpu.VMEM((TOK, D), F32),
            pltpu.VMEM((TOK, 1), F32),
            pltpu.VMEM((TOK, 2), F32),
            pltpu.VMEM((TOK, 1), F32),
            pltpu.VMEM((SLOTS, D), BF),
            pltpu.VMEM((SLOTS, D), BF),
            pltpu.VMEM((ROWS, D), BF),
            pltpu.VMEM((ROWS, D), BF),
            pltpu.VMEM((HID, D), BF),
            pltpu.VMEM((HID, D), BF),
            pltpu.VMEM((ROWS, HID), BF),
            pltpu.VMEM((ROWS, HID), F32),
            pltpu.VMEM((ROWS, HID), BF),
            pltpu.VMEM((HID, ROWS), BF),
        ]
        + [pltpu.VMEM((SLOTS, D), BF)] * 8
        + grad_scratch * 2
        + [
            dma((2, CUTS, NE)),
            dma((2, CUTS, NE)),
            dma((2, CUTS, 4)),
            dma((2, CUTS, 4)),
            dma((2, tiles)),
            dma((2, tiles)),
            dma((2, len(SPANS), NE)),
            dma((2, len(SPANS), NE)),
            dma((2, CUTS, 4)),
            dma((2, CUTS, 4)),
            dma((2, CUTS, 4)),
            dma((2, CUTS, 4)),
            dma((2, CUTS, 2, 4)),
            dma((2, CUTS, 2, 4)),
            dma((2, 2, tiles)),
            dma((2, 2, tiles)),
            dma((2, tiles)),
            dma((2, tiles)),
            dma((2, tiles, 4)),
            dma((2, tiles, 4)),
        ],
        compiler_params=pltpu.CompilerParams(
            collective_id=0, has_side_effects=True, vmem_limit_bytes=60 * 2**20
        ),
    )(tokens, cotangent, gate_weights.T, expert_ids.T, *rest)
    out, tg, gg, eg, rg = pl.pallas_call(
        hand_out,
        out_shape=shapes,
        in_specs=[hbm] * 5,
        out_specs=(hbm,) * 5,
        scratch_shapes=[pltpu.VMEM(one.shape, one.dtype) for one in shapes] + [dma((2, 5))],
    )(*results)
    return out, tg, gg.T, eg, rg


def solution(mesh):
    rows = P(("dp", "expert"), None)
    weights = P("expert", "dp", None)
    return jax.shard_map(
        body,
        mesh=mesh,
        in_specs=(rows,) * 6 + (weights,) * 2,
        out_specs=(rows,) * 3 + (weights,) * 2,
        check_vma=False,
    )
```
